32 devices in a mesh: blk: 16 (over z, y, core), tensor: 2 (over x).
Axes of the slice: x: 2, y: 2, z: 4, core: 2. Of those that a mesh axis runs over, the one named last changes fastest.
Arguments:
- activations: bfloat16 [6144, 5120], P('blk'), may hold values from -6 to 6
- out_grad: bfloat16 [6144, 5120], P('blk'), may hold values from -12 to 12
- gate_weight: bfloat16 [16, 5120, 108], P('blk', None, 'tensor'), may hold values from -0.078125 to 0.078125
- up_weight: bfloat16 [16, 5120, 108], P('blk', None, 'tensor'), may hold values from -0.078125 to 0.078125
- down_weight: bfloat16 [16, 108, 5120], P('blk', 'tensor'), may hold values from -0.625 to 0.625
Outputs:
- in_grad: bfloat16 [6144, 5120], P(('blk', 'tensor'))
- gate_accum: float32 [16, 5120, 108], P('blk', None, 'tensor')
- up_accum: float32 [16, 5120, 108], P('blk', None, 'tensor')
- down_accum: float32 [16, 108, 5120], P('blk', 'tensor')
The draws below stay inside these ranges and needn't reach their ends.
All inputs are finite; a program needn't handle non-finite values.
Results may differ from the reference program's by a relative error of at most 0.006.
Values may be sent and summed in bfloat16 or wider, within the bound.
No kernel may reach another device: no remote copies, remote signals or barrier semaphores. Data moves between devices by JAX's collectives and lax.ppermute only.
A program may use at most 128 MiB of HBM per device.

```python
import jax
import jax.numpy as jnp
from jax import lax

D = 5120
HB = 54
TOK_DEV = 384
BLOCKS = 16
TOKENS = 6144
FCOL = 108
N_BLK = 16


def steps_of(key, dims, cuts, low, high):
    def one(axis_at, blocks):
        heights = jax.random.uniform(jax.random.fold_in(jax.random.fold_in(key, 6), axis_at), (blocks,), jnp.float32, low / len(cuts), high / len(cuts))
        return jnp.repeat(jnp.exp(heights), dims[axis_at] // blocks).reshape((-1,) + (1,) * (len(dims) - axis_at - 1))

    loudness = one(*cuts[0])
    for cut in cuts[1:]:
        loudness = loudness * one(*cut)
    return loudness


def centred(stream_key, extent, width, limit, cuts=(), held_as=jnp.bfloat16):
    drawn = jax.random.normal(stream_key, extent, jnp.float32) * width
    if len(cuts) > 0:
        drawn = steps_of(stream_key, extent, cuts, -0.22, 0.18) * drawn
    return jnp.clip(drawn, min=-limit, max=limit).astype(held_as)


def setup_inputs(seed: int = 0) -> dict:
    key_of = jax.random.split(jax.random.key(seed), 6)
    return {
        "activations": centred(key_of[0], (TOKENS, D), 1.0, 6.0, ((0, 16),)),
        "out_grad": centred(key_of[1], (TOKENS, D), 2.0, 12.0, ((0, 16),)),
        "gate_weight": centred(key_of[2], (BLOCKS, D, FCOL), D ** -0.5, 0.078125, ((0, 16), (2, 2))),
        "up_weight": centred(key_of[3], (BLOCKS, D, FCOL), D ** -0.5, 0.078125, ((0, 16), (2, 2))),
        "down_weight": centred(key_of[4], (BLOCKS, FCOL, D), FCOL ** -0.5, 0.625, ((0, 16), (1, 2))),
    }


def pieces(rows_in, rows_grad, w_gate, w_up, w_down):
    gate_pre = jnp.dot(rows_in, w_gate, preferred_element_type=jnp.float32)
    up_pre = jnp.dot(rows_in, w_up, preferred_element_type=jnp.float32)
    sigmoid_part = jax.nn.sigmoid(gate_pre)
    silu_part = gate_pre * sigmoid_part
    hidden = (silu_part * up_pre).astype(jnp.bfloat16)
    grad_hidden = jnp.dot(rows_grad, w_down.T, preferred_element_type=jnp.float32)
    slope_part = sigmoid_part * (1.0 + gate_pre * (1.0 - sigmoid_part))
    grad_gate = (grad_hidden * up_pre * slope_part).astype(jnp.bfloat16)
    grad_up = (grad_hidden * silu_part).astype(jnp.bfloat16)
    return (hidden, grad_gate, grad_up)

def block_of(gate_weight, up_weight, down_weight, block):
    w_gate = lax.dynamic_index_in_dim(gate_weight, block, 0, keepdims=False)
    w_up = lax.dynamic_index_in_dim(up_weight, block, 0, keepdims=False)
    w_down = lax.dynamic_index_in_dim(down_weight, block, 0, keepdims=False)
    return (w_gate, w_up, w_down)

def rows_of(array, index):
    return lax.dynamic_slice_in_dim(array, index * TOK_DEV, TOK_DEV, 0)

def reference(activations, out_grad, gate_weight, up_weight, down_weight):
    n_tensor = FCOL // HB

    def input_grad(micro):
        rows_in = rows_of(activations, micro)
        rows_grad = rows_of(out_grad, micro)
        total = jnp.zeros((n_tensor, TOK_DEV, D), jnp.float32)
        for step in (0, 1):
            block = jnp.mod(micro - step, N_BLK).astype(jnp.int32)
            w_gate, w_up, w_down = block_of(gate_weight, up_weight, down_weight, block)
            hidden, grad_gate, grad_up = pieces(rows_in, rows_grad, w_gate, w_up, w_down)
            total = total + jnp.einsum('rth,dth->trd', grad_gate.astype(jnp.float32).reshape(TOK_DEV, n_tensor, HB), w_gate.astype(jnp.float32).reshape(D, n_tensor, HB), precision=lax.Precision.HIGHEST)
            total = total + jnp.einsum('rth,dth->trd', grad_up.astype(jnp.float32).reshape(TOK_DEV, n_tensor, HB), w_up.astype(jnp.float32).reshape(D, n_tensor, HB), precision=lax.Precision.HIGHEST)
        rounded = lax.optimization_barrier(total.astype(jnp.bfloat16))
        return lax.optimization_barrier(jnp.sum(rounded.astype(jnp.float32), axis=0)).astype(jnp.bfloat16)

    def accum(block):
        w_gate, w_up, w_down = block_of(gate_weight, up_weight, down_weight, block)
        acc_gate = jnp.zeros((D, FCOL), jnp.float32)
        acc_up = jnp.zeros((D, FCOL), jnp.float32)
        acc_down = jnp.zeros((FCOL, D), jnp.float32)
        for step in (0, 1):
            micro = jnp.mod(block + step, N_BLK).astype(jnp.int32)
            rows_in = rows_of(activations, micro)
            rows_grad = rows_of(out_grad, micro)
            hidden, grad_gate, grad_up = pieces(rows_in, rows_grad, w_gate, w_up, w_down)
            acc_gate = acc_gate + jnp.dot(rows_in.T, grad_gate, preferred_element_type=jnp.float32)
            acc_up = acc_up + jnp.dot(rows_in.T, grad_up, preferred_element_type=jnp.float32)
            acc_down = acc_down + jnp.dot(hidden.T, rows_grad, preferred_element_type=jnp.float32)
        return (acc_gate, acc_up, acc_down)
    indices = jnp.arange(N_BLK, dtype=jnp.int32)
    per_micro = lax.map(input_grad, indices)
    in_grad = per_micro.reshape(TOKENS, D)
    gate_accum, up_accum, down_accum = lax.map(accum, indices)
    return (in_grad, gate_accum, up_accum, down_accum)
```

```python
import jax
import jax.numpy as jnp
from jax import lax
from jax.sharding import PartitionSpec as P

F32 = jnp.float32
BF16 = jnp.bfloat16


def from_behind(value, axis, by):
    devices = lax.axis_size(axis)
    return lax.ppermute(value, axis, [(i, (i + by) % devices) for i in range(devices)])


def pre(rows, w):
    return lax.dot_general(w, rows, (((1,), (1,)), ((), ())), preferred_element_type=F32)


def terms(gate_pre, up_pre, grad_hidden):
    sigmoid_part = jax.nn.sigmoid(gate_pre)
    silu_part = gate_pre * sigmoid_part
    hidden = (silu_part * up_pre).astype(BF16)
    slope_part = sigmoid_part * (1.0 + gate_pre * (1.0 - sigmoid_part))
    grad_gate = (grad_hidden * up_pre * slope_part).astype(BF16)
    grad_up = (grad_hidden * silu_part).astype(BF16)
    return hidden, grad_gate, grad_up


def accum(term, rows):
    return jnp.dot(term, rows, preferred_element_type=F32)


def local(activations, out_grad, gate_weight, up_weight, down_weight):
    n_blk, n_tensor = lax.axis_size("blk"), lax.axis_size("tensor")
    w_gate, w_up, w_down = gate_weight[0].T, up_weight[0].T, down_weight[0]
    prev_down, prev_gate, prev_up = [from_behind(w, "blk", 1) for w in (w_down, w_gate, w_up)]
    pairs = n_tensor == 2 and n_blk % 2 == 0
    if pairs:
        swap = [(0, 1), (1, 0)]
        other_gate, other_up = [lax.ppermute(w, "tensor", swap) for w in (w_gate, w_up)]
        axes = ("blk", "tensor")
        on_chip = [(2 * b + j, 2 * (b + 1) + j) for b in range(0, n_blk, 2) for j in range(2)]
        across = [(2 * b + j, 2 * b + 1 - j) for b in range(0, n_blk, 2) for j in range(2)]
        prev_other = [
            lax.ppermute(mine, axes, on_chip) + lax.ppermute(prev, axes, across)
            for mine, prev in ((other_gate, prev_gate), (other_up, prev_up))
        ]
    own = terms(pre(activations, w_gate), pre(activations, w_up), pre(out_grad, w_down))
    prev = terms(pre(activations, prev_gate), pre(activations, prev_up), pre(out_grad, prev_down))
    rows_of = (out_grad, activations, activations)
    back = [from_behind(accum(t, r).astype(BF16), "blk", -1) for t, r in zip(prev, rows_of)]
    total_down, total_gate, total_up = [
        accum(t, r) + b.astype(F32) for t, r, b in zip(own, rows_of, back)
    ]
    grads = jnp.concatenate([own[1], own[2], prev[1], prev[2]], axis=0)
    if pairs:
        rows = activations.shape[0] // 2
        j = lax.axis_index("tensor")
        mine = lax.dynamic_slice_in_dim(grads, j * rows, rows, 1)
        theirs = lax.ppermute(lax.dynamic_slice_in_dim(grads, (1 - j) * rows, rows, 1), "tensor", swap)
        left = jnp.concatenate([mine, theirs], axis=0)
        right = jnp.concatenate(
            [w_gate, w_up, prev_gate, prev_up, other_gate, other_up] + prev_other, axis=0
        )
        in_grad = lax.dot_general(
            left, right, (((0,), (0,)), ((), ())), preferred_element_type=F32
        ).astype(BF16)
    else:
        right = jnp.concatenate([w_gate, w_up, prev_gate, prev_up], axis=0)
        partial = lax.dot_general(
            grads, right, (((0,), (0,)), ((), ())), preferred_element_type=F32
        ).astype(BF16)
        in_grad = lax.psum_scatter(partial, "tensor", scatter_dimension=0, tiled=True)
    return in_grad, total_gate.T[None], total_up.T[None], total_down[None]


def solution(mesh):
    in_specs = (
        P("blk", None),
        P("blk", None),
        P("blk", None, "tensor"),
        P("blk", None, "tensor"),
        P("blk", "tensor", None),
    )
    out_specs = (
        P(("blk", "tensor"), None),
        P("blk", None, "tensor"),
        P("blk", None, "tensor"),
        P("blk", "tensor", None),
    )
    return jax.shard_map(local, mesh=mesh, in_specs=in_specs, out_specs=out_specs, check_vma=False)
```

```python
import functools

import jax
import jax.numpy as jnp
from jax import lax
from jax.experimental import pallas as pl
from jax.experimental.pallas import tpu as pltpu
from jax.sharding import PartitionSpec as P

F32 = jnp.float32
BF16 = jnp.bfloat16
VMEM_LIMIT = 32 * 2**20


def from_behind(value, axis, by):
    devices = lax.axis_size(axis)
    return lax.ppermute(value, axis, [(i, (i + by) % devices) for i in range(devices)])


def pre(rows, w):
    return lax.dot_general(w, rows, (((1,), (1,)), ((), ())), preferred_element_type=F32)


def terms(gate_pre, up_pre, grad_hidden):
    sigmoid_part = jax.nn.sigmoid(gate_pre)
    silu_part = gate_pre * sigmoid_part
    hidden = (silu_part * up_pre).astype(BF16)
    slope_part = sigmoid_part * (1.0 + gate_pre * (1.0 - sigmoid_part))
    grad_gate = (grad_hidden * up_pre * slope_part).astype(BF16)
    grad_up = (grad_hidden * silu_part).astype(BF16)
    return hidden, grad_gate, grad_up


def accum(term, rows):
    return jnp.dot(term, rows, preferred_element_type=F32)


def column_block(width, limit):
    block = limit
    while width % block:
        block -= 128
    return block


def total_kernel(own_ref, back_ref, out_ref):
    out_ref[:, 0, :] = own_ref[...] + back_ref[...].astype(F32)


def total(own, back):
    hidden, width = own.shape
    block = column_block(width, 1280)
    return pl.pallas_call(
        total_kernel,
        grid=(width // block,),
        in_specs=[pl.BlockSpec((hidden, block), lambda i: (0, i))] * 2,
        out_specs=pl.BlockSpec((hidden, 1, block), lambda i: (0, 0, i)),
        out_shape=jax.ShapeDtypeStruct((hidden, 1, width), F32),
        compiler_params=pltpu.CompilerParams(vmem_limit_bytes=VMEM_LIMIT),
        cost_estimate=pl.CostEstimate(
            flops=hidden * width, bytes_accessed=10 * hidden * width, transcendentals=0
        ),
        name="total",
    )(own, back)


def in_grad_kernel(n, groups, *refs):
    left_refs, right_refs = refs[:n], refs[n:-3]
    out_ref, left_scr, right_scr = refs[-3:]
    hidden = left_refs[0].shape[1]
    step = left_scr.shape[0] // left_refs[0].shape[0]

    @pl.when(pl.program_id(0) == 0)
    def _():
        left_scr[...] = jnp.zeros_like(left_scr)
        right_scr[...] = jnp.zeros_like(right_scr)

    result = None
    at = 0
    for left_ref in left_refs:
        for k in range(left_ref.shape[0]):
            left_scr[pl.ds(k * step, hidden), :] = left_ref[k]
            right = right_refs[at][...]
            for more in right_refs[at + 1 : at + groups[k]]:
                right = right + more[...]
            at += groups[k]
            right_scr[pl.ds(k * step, hidden), :] = right
        partial = lax.dot_general(
            left_scr[...], right_scr[...], (((0,), (0,)), ((), ())), preferred_element_type=F32
        )
        partial = partial.astype(BF16).astype(F32)
        result = partial if result is None else result + partial
        groups = groups[left_ref.shape[0] :]
    out_ref[...] = result.astype(BF16)


def in_grad_of(lefts, rights):
    count, hidden, rows = lefts[0].shape
    groups = [len(r) for r in rights]
    flat = [t for r in rights for t in r]
    width = flat[0].shape[1]
    block = column_block(width, 1280)
    step = -(-hidden // 64) * 64
    return pl.pallas_call(
        functools.partial(in_grad_kernel, len(lefts), groups),
        grid=(width // block,),
        in_specs=[pl.BlockSpec(l.shape, lambda i: (0, 0, 0)) for l in lefts]
        + [pl.BlockSpec((hidden, block), lambda i: (0, i))] * len(flat),
        out_specs=pl.BlockSpec((rows, block), lambda i: (0, i)),
        out_shape=jax.ShapeDtypeStruct((rows, width), BF16),
        scratch_shapes=[
            pltpu.VMEM((count * step, rows), BF16),
            pltpu.VMEM((count * step, block), BF16),
        ],
        compiler_params=pltpu.CompilerParams(vmem_limit_bytes=VMEM_LIMIT),
        cost_estimate=pl.CostEstimate(
            flops=2 * len(rights) * hidden * rows * width,
            bytes_accessed=2 * width * (rows + len(flat) * hidden),
            transcendentals=0,
        ),
        name="in_grad",
    )(*lefts, *flat)


def local(activations, out_grad, gate_weight, up_weight, down_weight):
    n_blk, n_tensor = lax.axis_size("blk"), lax.axis_size("tensor")
    w_gate, w_up, w_down = gate_weight[0].T, up_weight[0].T, down_weight[0]
    prev_down, prev_gate, prev_up = [from_behind(w, "blk", 1) for w in (w_down, w_gate, w_up)]
    pairs = n_tensor == 2 and n_blk % 2 == 0
    if pairs:
        swap = [(0, 1), (1, 0)]
        other_gate, other_up = [lax.ppermute(w, "tensor", swap) for w in (w_gate, w_up)]
        axes = ("blk", "tensor")
        on_chip = [(2 * b + j, 2 * (b + 1) + j) for b in range(0, n_blk, 2) for j in range(2)]
        across = [(2 * b + j, 2 * b + 1 - j) for b in range(0, n_blk, 2) for j in range(2)]
        prev_other = [
            [lax.ppermute(mine, axes, on_chip), lax.ppermute(prev, axes, across)]
            for mine, prev in ((other_gate, prev_gate), (other_up, prev_up))
        ]
    own = terms(pre(activations, w_gate), pre(activations, w_up), pre(out_grad, w_down))
    prev = terms(pre(activations, prev_gate), pre(activations, prev_up), pre(out_grad, prev_down))
    rows_of = (out_grad, activations, activations)
    back = [from_behind(accum(t, r).astype(BF16), "blk", -1) for t, r in zip(prev, rows_of)]
    total_down, total_gate, total_up = [
        total(accum(t, r), b) for t, r, b in zip(own, rows_of, back)
    ]
    grads = jnp.stack([own[1], own[2], prev[1], prev[2]])
    if pairs:
        half = activations.shape[0] // 2
        first = lax.axis_index("tensor") == 0
        low, high = grads[:, :, :half], grads[:, :, half:]
        mine = jnp.where(first, low, high)
        theirs = lax.ppermute(jnp.where(first, high, low), "tensor", swap)
        in_grad = in_grad_of(
            [mine, theirs],
            [[w_gate], [w_up], [prev_gate], [prev_up], [other_gate], [other_up]] + prev_other,
        )
    else:
        partial = in_grad_of([grads], [[w_gate], [w_up], [prev_gate], [prev_up]])
        in_grad = lax.psum_scatter(partial, "tensor", scatter_dimension=0, tiled=True)
    return (
        in_grad,
        total_gate.transpose(1, 2, 0),
        total_up.transpose(1, 2, 0),
        total_down.transpose(1, 0, 2),
    )


def solution(mesh):
    in_specs = (
        P("blk", None),
        P("blk", None),
        P("blk", None, "tensor"),
        P("blk", None, "tensor"),
        P("blk", "tensor", None),
    )
    out_specs = (
        P(("blk", "tensor"), None),
        P("blk", None, "tensor"),
        P("blk", None, "tensor"),
        P("blk", "tensor", None),
    )
    return jax.shard_map(local, mesh=mesh, in_specs=in_specs, out_specs=out_specs, check_vma=False)
```

```python
import functools

import jax
import jax.numpy as jnp
from jax import lax
from jax.experimental import pallas as pl
from jax.experimental.pallas import tpu as pltpu
from jax.sharding import PartitionSpec as P

F32 = jnp.float32
BF16 = jnp.bfloat16
VMEM_LIMIT = 16 * 2**20
VMEM = pl.BlockSpec(memory_space=pltpu.VMEM)
ANY = pl.BlockSpec(memory_space=pl.ANY)
HBM = pl.BlockSpec(memory_space=pltpu.HBM)
SMEM = pl.BlockSpec(memory_space=pltpu.SMEM)


def from_behind(value, axis, by):
    devices = lax.axis_size(axis)
    return lax.ppermute(value, axis, [(i, (i + by) % devices) for i in range(devices)])


def column_block(width, limit):
    block = limit
    while width % block:
        block -= 128
    return block


def columns(width, limit=1280):
    block = column_block(width, limit)
    return [pl.ds(at, block) for at in range(0, width, block)]


def in_vmem(*arrays):
    return [pltpu.with_memory_space_constraint(a, pltpu.VMEM) for a in arrays]


def params(flops, nbytes):
    return dict(
        compiler_params=pltpu.CompilerParams(vmem_limit_bytes=VMEM_LIMIT),
        cost_estimate=pl.CostEstimate(flops=flops, bytes_accessed=nbytes, transcendentals=0),
    )


def stacked(gate, up, step):
    if gate.shape[0] == step:
        return jnp.concatenate([gate, up], axis=0)
    pad = jnp.zeros((step - gate.shape[0], gate.shape[1]), gate.dtype)
    return jnp.concatenate([gate, pad, up, pad], axis=0)


def pre_of(stack_ref, gate_ref, up_ref, rows_ref):
    total = None
    for at in columns(stack_ref.shape[1]):
        weight = stacked(gate_ref[:, at], up_ref[:, at], stack_ref.shape[0] // 2)
        stack_ref[:, at] = weight
        term = lax.dot_general(
            weight, rows_ref[:, at], (((1,), (1,)), ((), ())), preferred_element_type=F32
        )
        total = term if total is None else total + term
    return total


def hidden_of(pre):
    step = pre.shape[0] // 2
    gate_pre, up_pre = pre[:step], pre[step:]
    return (gate_pre * jax.nn.sigmoid(gate_pre) * up_pre).astype(BF16)


def product(weight_ref, rows_ref):
    total = None
    for at in columns(weight_ref.shape[1]):
        term = lax.dot_general(
            weight_ref[:, at], rows_ref[:, at], (((1,), (1,)), ((), ())), preferred_element_type=F32
        )
        total = term if total is None else total + term
    return total


def grads_of(pre, grad_hidden):
    step, hidden = pre.shape[0] // 2, grad_hidden.shape[0]
    if step > hidden:
        pad = jnp.zeros((step - hidden, grad_hidden.shape[1]), F32)
        grad_hidden = jnp.concatenate([grad_hidden, pad], axis=0)
    gate_pre, up_pre = pre[:step], pre[step:]
    sigmoid_part = jax.nn.sigmoid(gate_pre)
    slope_part = sigmoid_part * (1.0 + gate_pre * (1.0 - sigmoid_part))
    grad_gate = (grad_hidden * up_pre * slope_part).astype(BF16)
    grad_up = (grad_hidden * (gate_pre * sigmoid_part)).astype(BF16)
    return jnp.concatenate([grad_gate, grad_up], axis=0)


def terms_of(early_ref, late_ref, hidden, grads, x_ref, g_ref):
    step = hidden.shape[0]
    for at in columns(x_ref.shape[1]):
        down = jnp.dot(hidden, g_ref[:, at], preferred_element_type=F32)
        gate_up = jnp.dot(grads, x_ref[:, at], preferred_element_type=F32)
        early = jnp.concatenate([down, gate_up[:step]], axis=0)
        early_ref[:, at] = early.astype(early_ref.dtype)
        late_ref[:, at] = gate_up[step:].astype(late_ref.dtype)


def own_kernel(x_ref, g_ref, gate_in, up_in, down_in, stack_ref, grads_ref, hidden_ref, gate_ref, up_ref, down_ref, sem):
    copies = [
        pltpu.make_async_copy(source, into, sem.at[n])
        for n, (source, into) in enumerate(
            [(gate_in, gate_ref), (up_in, up_ref), (down_in, down_ref)]
        )
    ]
    for copy in copies:
        copy.start()
    copies[0].wait()
    copies[1].wait()
    pre = pre_of(stack_ref, gate_ref, up_ref, x_ref)
    hidden_ref[...] = hidden_of(pre)
    copies[2].wait()
    grads_ref[...] = grads_of(pre, product(down_ref, g_ref))


def own_meeting(x, g, w_gate, w_up, w_down, step):
    rows, width = x.shape
    weights = [pltpu.with_memory_space_constraint(w, pltpu.HBM) for w in (w_gate, w_up, w_down)]
    return pl.pallas_call(
        own_kernel,
        in_specs=[VMEM] * 2 + [HBM] * 3,
        out_specs=[VMEM] * 3,
        out_shape=[
            pltpu.VMEM((2 * step, width), BF16),
            pltpu.VMEM((2 * step, rows), BF16),
            pltpu.VMEM((step, rows), BF16),
        ],
        scratch_shapes=[pltpu.VMEM(w_gate.shape, BF16)] * 3 + [pltpu.SemaphoreType.DMA((3,))],
        name="own_meeting",
        **params(6 * step * rows * width, 4 * rows * width),
    )(*in_vmem(x, g), *weights)


def grad_hidden_kernel(g_ref, down_ref, after_ref, out_ref):
    del after_ref
    out_ref[...] = product(down_ref, g_ref)


def grad_hidden_of(g, w_down, after):
    rows, width = g.shape
    return pl.pallas_call(
        grad_hidden_kernel,
        in_specs=[VMEM] * 2 + [ANY],
        out_specs=VMEM,
        out_shape=pltpu.VMEM((w_down.shape[0], rows), F32),
        name="grad_hidden",
        **params(2 * w_down.size * rows, 2 * g.size),
    )(*in_vmem(g, w_down), after)


def second_kernel(n_stacks, halves, x_ref, g_ref, prev_ref, own_ref, index_ref, *refs):
    weights, (early_ref, late_ref, *refs) = refs[: 2 * n_stacks], refs[2 * n_stacks :]
    stack_refs, grads_refs = refs[:n_stacks], refs[n_stacks:]
    step = late_ref.shape[0]
    pre = pre_of(stack_refs[0], weights[0], weights[1], x_ref)
    grads = grads_of(pre, prev_ref[...])
    terms_of(early_ref, late_ref, hidden_of(pre), grads, x_ref, g_ref)
    both = jnp.concatenate([own_ref[...], grads], axis=0)
    if halves == 1:
        grads_refs[0][...] = both
        return
    half = both.shape[1] // 2

    @pl.when(index_ref[0] == 0)
    def _():
        grads_refs[0][...] = both[:, :half]
        grads_refs[1][...] = both[:, half:]

    @pl.when(index_ref[0] != 0)
    def _():
        grads_refs[0][...] = both[:, half:]
        grads_refs[1][...] = both[:, :half]

    for n in range(1, n_stacks):
        for at in columns(x_ref.shape[1]):
            gate, up = weights[2 * n][:, at], weights[2 * n + 1][:, at]
            stack_refs[n][:, at] = stacked(gate, up, step)


def second_meeting(x, g, grad_hidden, own_grads, weights, index, halves):
    rows, width = x.shape
    step2 = own_grads.shape[0]
    n_stacks = len(weights) // 2
    return pl.pallas_call(
        functools.partial(second_kernel, n_stacks, halves),
        in_specs=[VMEM] * 4 + [SMEM] + [VMEM] * len(weights),
        out_specs=[VMEM] * (2 + n_stacks + halves),
        out_shape=[pltpu.VMEM((step2, width), BF16), pltpu.VMEM((step2 // 2, width), BF16)]
        + [pltpu.VMEM((step2, width), BF16)] * n_stacks
        + [pltpu.VMEM((2 * step2, rows // halves), BF16)] * halves,
        name="second_meeting",
        **params(6 * step2 * rows * width, 4 * rows * width),
    )(*in_vmem(x, g, grad_hidden, own_grads), index.reshape(1), *in_vmem(*weights))


def stack_kernel(gate_ref, up_ref, after_ref, out_ref):
    del after_ref
    for at in columns(out_ref.shape[1]):
        out_ref[:, at] = stacked(gate_ref[:, at], up_ref[:, at], out_ref.shape[0] // 2)


def stack(w_gate, w_up, step, after):
    width = w_gate.shape[1]
    return pl.pallas_call(
        stack_kernel,
        in_specs=[VMEM, VMEM, ANY],
        out_specs=VMEM,
        out_shape=pltpu.VMEM((2 * step, width), BF16),
        name="stack",
        **params(0, 8 * step * width),
    )(*in_vmem(w_gate, w_up), after)


def sums_kernel(x_ref, g_ref, hidden_ref, grads_ref, after_ref, early_ref, late_ref):
    del after_ref
    terms_of(early_ref, late_ref, hidden_ref[...], grads_ref[...], x_ref, g_ref)


def own_sums(x, g, hidden, grads, after):
    rows, width = x.shape
    return pl.pallas_call(
        sums_kernel,
        in_specs=[VMEM] * 4 + [ANY],
        out_specs=[VMEM] * 2,
        out_shape=[pltpu.VMEM((n * hidden.shape[0], width), F32) for n in (2, 1)],
        name="own_sums",
        **params(6 * hidden.shape[0] * rows * width, 4 * rows * width),
    )(*in_vmem(x, g, hidden, grads), after)


def total_kernel(own_in, back_in, after_ref, *refs):
    del after_ref
    out_refs, (own_ref, back_ref, in_sem, out_sem) = refs[:-4], refs[-4:]
    step, hidden = own_ref.shape[0] // len(out_refs), out_refs[0].shape[0]
    rows = [pl.ds(k * step, step) for k in range(len(out_refs))]
    loads = [pltpu.make_async_copy(back_in, back_ref, in_sem.at[0])] + [
        pltpu.make_async_copy(own_in.at[at, :], own_ref.at[at, :], in_sem.at[1 + k])
        for k, at in enumerate(rows)
    ]
    for copy in loads:
        copy.start()
    loads[0].wait()
    stores = []
    for k, at in enumerate(rows):
        loads[1 + k].wait()
        for first in range(0, step, 8):
            part = pl.ds(k * step + first, 8)
            own_ref[part, :] = own_ref[part, :] + back_ref[part, :].astype(F32)
            for r in range(first, min(first + 8, hidden)):
                row = own_ref.at[pl.ds(k * step + r, 1), :]
                stores.append(pltpu.make_async_copy(row, out_refs[k].at[r], out_sem.at[k, r]))
                stores[-1].start()
    for copy in stores:
        copy.wait()


def totals(own, back, count, hidden, after):
    rows, width = own.shape
    return pl.pallas_call(
        total_kernel,
        in_specs=[ANY] * 3,
        out_specs=[HBM] * count,
        out_shape=[jax.ShapeDtypeStruct((hidden, 1, width), F32)] * count,
        scratch_shapes=[
            pltpu.VMEM((rows, width), F32),
            pltpu.VMEM((rows, width), BF16),
            pltpu.SemaphoreType.DMA((1 + count,)),
            pltpu.SemaphoreType.DMA((count, hidden)),
        ],
        name="totals",
        **params(rows * width, 10 * rows * width),
    )(own, back, after)


def in_grad_kernel(left_counts, right_counts, after_ref, *refs):
    del after_ref
    *refs, out_ref, scratch, sem = refs
    stores = []
    for n, at in enumerate(columns(out_ref.shape[1])):
        rest = list(refs)
        result = None
        for n_left, groups in zip(left_counts, right_counts):
            left = [rest.pop(0)[...] for _ in range(n_left)]
            right = []
            for count in groups:
                term = rest.pop(0)[:, at]
                for _ in range(count - 1):
                    term = term + rest.pop(0)[:, at]
                right.append(term)
            partial = lax.dot_general(
                jnp.concatenate(left, axis=0),
                jnp.concatenate(right, axis=0),
                (((0,), (0,)), ((), ())),
                preferred_element_type=F32,
            )
            partial = partial.astype(BF16).astype(F32)
            result = partial if result is None else result + partial
        scratch[:, at] = result.astype(BF16)
        stores.append(pltpu.make_async_copy(scratch.at[:, at], out_ref.at[:, at], sem.at[n]))
        stores[-1].start()
    for copy in stores:
        copy.wait()


def in_grad_of(after, *partials):
    operands = []
    for lefts, rights in partials:
        operands += lefts + [t for r in rights for t in r]
    rows, width = partials[0][0][0].shape[1], partials[0][1][0][0].shape[1]
    return pl.pallas_call(
        functools.partial(
            in_grad_kernel,
            [len(l) for l, _ in partials],
            [[len(t) for t in r] for _, r in partials],
        ),
        in_specs=[ANY] + [VMEM] * len(operands),
        out_specs=HBM,
        out_shape=jax.ShapeDtypeStruct((rows, width), BF16),
        scratch_shapes=[
            pltpu.VMEM((rows, width), BF16),
            pltpu.SemaphoreType.DMA((len(columns(width)),)),
        ],
        name="in_grad",
        **params(
            2 * sum(t.shape[0] for l, _ in partials for t in l) * rows * width,
            2 * sum(t.size for t in operands) + 2 * rows * width,
        ),
    )(after, *in_vmem(*operands))


def local(activations, out_grad, gate_weight, up_weight, down_weight):
    n_blk, n_tensor = lax.axis_size("blk"), lax.axis_size("tensor")
    hidden = gate_weight.shape[2]
    step = -(-hidden // 8) * 8
    pairs = n_tensor == 2 and n_blk % 2 == 0
    w_gate, w_up, w_down = gate_weight[0].T, up_weight[0].T, down_weight[0]
    prev_down, prev_gate, prev_up = [from_behind(w, "blk", 1) for w in (w_down, w_gate, w_up)]
    weights = [prev_gate, prev_up]
    if pairs:
        axes = ("blk", "tensor")
        swap = [(0, 1), (1, 0)]
        on_chip = [(2 * b + j, 2 * (b + 1) + j) for b in range(0, n_blk, 2) for j in range(2)]
        across = [(2 * b + j, 2 * b + 1 - j) for b in range(0, n_blk, 2) for j in range(2)]
        other_gate, other_up = [lax.ppermute(w, "tensor", swap) for w in (w_gate, w_up)]

    w_gu, own_grads, own_hidden = own_meeting(activations, out_grad, w_gate, w_up, w_down, step)
    grad_hidden = grad_hidden_of(out_grad, prev_down, own_grads)
    early, late, prev_gu, *grads = second_meeting(
        activations,
        out_grad,
        grad_hidden,
        own_grads,
        weights,
        lax.axis_index("tensor"),
        2 if pairs else 1,
    )
    back_early, back_late = [from_behind(t, "blk", -1) for t in (early, late)]
    sums_early, sums_late = own_sums(activations, out_grad, own_hidden, own_grads, prev_gu)
    total_down, total_gate = totals(sums_early, back_early, 2, hidden, prev_gu)
    if pairs:
        mine, sent = grads
        prev_other_even = lax.ppermute(prev_gu, axes, across)
        theirs = lax.ppermute(sent, "tensor", swap)
        other_gu = stack(other_gate, other_up, step, theirs)
        prev_other_odd = lax.ppermute(other_gu, axes, on_chip)
        in_grad = in_grad_of(
            total_gate,
            ([mine], [[w_gu], [prev_gu]]),
            ([theirs], [[other_gu], [prev_other_even, prev_other_odd]]),
        )
        after = in_grad
    else:
        after = in_grad_of(prev_gu, (grads, [[w_gu], [prev_gu]]))
        in_grad = lax.psum_scatter(after, "tensor", scatter_dimension=0, tiled=True)
    [total_up] = totals(sums_late, back_late, 1, hidden, after)
    return (
        in_grad,
        total_gate.transpose(1, 2, 0),
        total_up.transpose(1, 2, 0),
        total_down.transpose(1, 0, 2),
    )


def solution(mesh):
    in_specs = (
        P("blk", None),
        P("blk", None),
        P("blk", None, "tensor"),
        P("blk", None, "tensor"),
        P("blk", "tensor", None),
    )
    out_specs = (
        P(("blk", "tensor"), None),
        P("blk", None, "tensor"),
        P("blk", None, "tensor"),
        P("blk", "tensor", None),
    )
    return jax.shard_map(local, mesh=mesh, in_specs=in_specs, out_specs=out_specs, check_vma=False)
```

```python
import functools

import jax
import jax.numpy as jnp
from jax import lax
from jax.experimental import pallas as pl
from jax.experimental.pallas import tpu as pltpu
from jax.sharding import PartitionSpec as P

F32 = jnp.float32
BF16 = jnp.bfloat16
VMEM_LIMIT = 16 * 2**20
VMEM = pl.BlockSpec(memory_space=pltpu.VMEM)
ANY = pl.BlockSpec(memory_space=pl.ANY)
HBM = pl.BlockSpec(memory_space=pltpu.HBM)
SMEM = pl.BlockSpec(memory_space=pltpu.SMEM)


def from_behind(value, axis, by):
    devices = lax.axis_size(axis)
    return lax.ppermute(value, axis, [(i, (i + by) % devices) for i in range(devices)])


def column_block(width, limit):
    block = limit
    while width % block:
        block -= 128
    return block


def columns(width, limit=1280):
    block = column_block(width, limit)
    return [pl.ds(at, block) for at in range(0, width, block)]


def in_vmem(*arrays):
    return [pltpu.with_memory_space_constraint(a, pltpu.VMEM) for a in arrays]


def params(flops, nbytes):
    return dict(
        compiler_params=pltpu.CompilerParams(vmem_limit_bytes=VMEM_LIMIT),
        cost_estimate=pl.CostEstimate(flops=flops, bytes_accessed=nbytes, transcendentals=0),
    )


def stacked(gate, up, step):
    if gate.shape[0] == step:
        return jnp.concatenate([gate, up], axis=0)
    pad = jnp.zeros((step - gate.shape[0], gate.shape[1]), gate.dtype)
    return jnp.concatenate([gate, pad, up, pad], axis=0)


def pre_of(stack_ref, gate_ref, up_ref, rows_ref):
    total = None
    for at in columns(stack_ref.shape[1]):
        weight = stacked(gate_ref[:, at], up_ref[:, at], stack_ref.shape[0] // 2)
        stack_ref[:, at] = weight
        term = lax.dot_general(
            weight, rows_ref[:, at], (((1,), (1,)), ((), ())), preferred_element_type=F32
        )
        total = term if total is None else total + term
    return total


def hidden_of(pre):
    step = pre.shape[0] // 2
    gate_pre, up_pre = pre[:step], pre[step:]
    return (gate_pre * jax.nn.sigmoid(gate_pre) * up_pre).astype(BF16)


def product(weight_ref, rows_ref):
    total = None
    for at in columns(weight_ref.shape[1]):
        term = lax.dot_general(
            weight_ref[:, at], rows_ref[:, at], (((1,), (1,)), ((), ())), preferred_element_type=F32
        )
        total = term if total is None else total + term
    return total


def grads_of(pre, grad_hidden):
    step, hidden = pre.shape[0] // 2, grad_hidden.shape[0]
    if step > hidden:
        pad = jnp.zeros((step - hidden, grad_hidden.shape[1]), F32)
        grad_hidden = jnp.concatenate([grad_hidden, pad], axis=0)
    gate_pre, up_pre = pre[:step], pre[step:]
    sigmoid_part = jax.nn.sigmoid(gate_pre)
    slope_part = sigmoid_part * (1.0 + gate_pre * (1.0 - sigmoid_part))
    grad_gate = (grad_hidden * up_pre * slope_part).astype(BF16)
    grad_up = (grad_hidden * (gate_pre * sigmoid_part)).astype(BF16)
    return jnp.concatenate([grad_gate, grad_up], axis=0)


def terms_of(early_ref, late_ref, hidden, grads, x_ref, g_ref):
    step = hidden.shape[0]
    for at in columns(x_ref.shape[1]):
        down = jnp.dot(hidden, g_ref[:, at], preferred_element_type=F32)
        gate_up = jnp.dot(grads, x_ref[:, at], preferred_element_type=F32)
        early = jnp.concatenate([down, gate_up[:step]], axis=0)
        early_ref[:, at] = early.astype(early_ref.dtype)
        late_ref[:, at] = gate_up[step:].astype(late_ref.dtype)


def own_kernel(x_ref, g_ref, gate_in, up_in, down_in, stack_ref, grads_ref, hidden_ref, gate_ref, up_ref, down_ref, sem):
    copies = [
        pltpu.make_async_copy(source, into, sem.at[n])
        for n, (source, into) in enumerate(
            [(gate_in, gate_ref), (up_in, up_ref), (down_in, down_ref)]
        )
    ]
    for copy in copies:
        copy.start()
    copies[0].wait()
    copies[1].wait()
    pre = pre_of(stack_ref, gate_ref, up_ref, x_ref)
    hidden_ref[...] = hidden_of(pre)
    copies[2].wait()
    grads_ref[...] = grads_of(pre, product(down_ref, g_ref))


def own_meeting(x, g, w_gate, w_up, w_down, step):
    rows, width = x.shape
    weights = [pltpu.with_memory_space_constraint(w, pltpu.HBM) for w in (w_gate, w_up, w_down)]
    return pl.pallas_call(
        own_kernel,
        in_specs=[VMEM] * 2 + [HBM] * 3,
        out_specs=[VMEM] * 3,
        out_shape=[
            pltpu.VMEM((2 * step, width), BF16),
            pltpu.VMEM((2 * step, rows), BF16),
            pltpu.VMEM((step, rows), BF16),
        ],
        scratch_shapes=[pltpu.VMEM(w_gate.shape, BF16)] * 3 + [pltpu.SemaphoreType.DMA((3,))],
        name="own_meeting",
        **params(6 * step * rows * width, 4 * rows * width),
    )(*in_vmem(x, g), *weights)


def grad_hidden_kernel(g_ref, down_ref, after_ref, out_ref):
    del after_ref
    out_ref[...] = product(down_ref, g_ref)


def grad_hidden_of(g, w_down, after):
    rows, width = g.shape
    return pl.pallas_call(
        grad_hidden_kernel,
        in_specs=[VMEM] * 2 + [ANY],
        out_specs=VMEM,
        out_shape=pltpu.VMEM((w_down.shape[0], rows), F32),
        name="grad_hidden",
        **params(2 * w_down.size * rows, 2 * g.size),
    )(*in_vmem(g, w_down), after)


def second_kernel(n_stacks, halves, x_ref, g_ref, prev_ref, own_ref, index_ref, *refs):
    weights, (early_ref, late_ref, *refs) = refs[: 2 * n_stacks], refs[2 * n_stacks :]
    stack_refs, grads_refs = refs[:n_stacks], refs[n_stacks:]
    step = late_ref.shape[0]
    pre = pre_of(stack_refs[0], weights[0], weights[1], x_ref)
    grads = grads_of(pre, prev_ref[...])
    terms_of(early_ref, late_ref, hidden_of(pre), grads, x_ref, g_ref)
    both = jnp.concatenate([own_ref[...], grads], axis=0)
    if halves == 1:
        grads_refs[0][...] = both
        return
    half = both.shape[1] // 2

    @pl.when(index_ref[0] == 0)
    def _():
        grads_refs[0][...] = both[:, :half]
        grads_refs[1][...] = both[:, half:]

    @pl.when(index_ref[0] != 0)
    def _():
        grads_refs[0][...] = both[:, half:]
        grads_refs[1][...] = both[:, :half]

    for n in range(1, n_stacks):
        for at in columns(x_ref.shape[1]):
            gate, up = weights[2 * n][:, at], weights[2 * n + 1][:, at]
            stack_refs[n][:, at] = stacked(gate, up, step)


def second_meeting(x, g, grad_hidden, own_grads, weights, index, halves):
    rows, width = x.shape
    step2 = own_grads.shape[0]
    n_stacks = len(weights) // 2
    return pl.pallas_call(
        functools.partial(second_kernel, n_stacks, halves),
        in_specs=[VMEM] * 4 + [SMEM] + [VMEM] * len(weights),
        out_specs=[VMEM] * (2 + n_stacks + halves),
        out_shape=[pltpu.VMEM((step2, width), BF16), pltpu.VMEM((step2 // 2, width), BF16)]
        + [pltpu.VMEM((step2, width), BF16)] * n_stacks
        + [pltpu.VMEM((2 * step2, rows // halves), BF16)] * halves,
        name="second_meeting",
        **params(6 * step2 * rows * width, 4 * rows * width),
    )(*in_vmem(x, g, grad_hidden, own_grads), index.reshape(1), *in_vmem(*weights))


def stack_kernel(gate_ref, up_ref, after_ref, out_ref):
    del after_ref
    for at in columns(out_ref.shape[1]):
        out_ref[:, at] = stacked(gate_ref[:, at], up_ref[:, at], out_ref.shape[0] // 2)


def stack(w_gate, w_up, step, after):
    width = w_gate.shape[1]
    return pl.pallas_call(
        stack_kernel,
        in_specs=[VMEM, VMEM, ANY],
        out_specs=VMEM,
        out_shape=pltpu.VMEM((2 * step, width), BF16),
        name="stack",
        **params(0, 8 * step * width),
    )(*in_vmem(w_gate, w_up), after)


def sums_kernel(x_ref, g_ref, hidden_ref, grads_ref, after_ref, early_ref, late_ref):
    del after_ref
    terms_of(early_ref, late_ref, hidden_ref[...], grads_ref[...], x_ref, g_ref)


def own_sums(x, g, hidden, grads, after):
    rows, width = x.shape
    return pl.pallas_call(
        sums_kernel,
        in_specs=[VMEM] * 4 + [ANY],
        out_specs=[VMEM] * 2,
        out_shape=[pltpu.VMEM((n * hidden.shape[0], width), F32) for n in (2, 1)],
        name="own_sums",
        **params(6 * hidden.shape[0] * rows * width, 4 * rows * width),
    )(*in_vmem(x, g, hidden, grads), after)


def total_kernel(own_in, back_in, after_ref, *refs):
    del after_ref
    out_refs, (own_ref, back_ref, in_sem, out_sem) = refs[:-4], refs[-4:]
    step, hidden = own_ref.shape[0] // len(out_refs), out_refs[0].shape[0]
    rows = [pl.ds(k * step, step) for k in range(len(out_refs))]
    loads = [pltpu.make_async_copy(back_in, back_ref, in_sem.at[0])] + [
        pltpu.make_async_copy(own_in.at[at, :], own_ref.at[at, :], in_sem.at[1 + k])
        for k, at in enumerate(rows)
    ]
    for copy in loads:
        copy.start()
    loads[0].wait()
    stores = []
    for k, at in enumerate(rows):
        loads[1 + k].wait()
        for first in range(0, step, 8):
            part = pl.ds(k * step + first, 8)
            own_ref[part, :] = own_ref[part, :] + back_ref[part, :].astype(F32)
            for r in range(first, min(first + 8, hidden)):
                row = own_ref.at[pl.ds(k * step + r, 1), :]
                stores.append(pltpu.make_async_copy(row, out_refs[k].at[r], out_sem.at[k, r]))
                stores[-1].start()
    for copy in stores:
        copy.wait()


def totals(own, back, count, hidden, after):
    rows, width = own.shape
    return pl.pallas_call(
        total_kernel,
        in_specs=[ANY, ANY, HBM],
        out_specs=[HBM] * count,
        out_shape=[jax.ShapeDtypeStruct((hidden, 1, width), F32)] * count,
        scratch_shapes=[
            pltpu.VMEM((rows, width), F32),
            pltpu.VMEM((rows, width), BF16),
            pltpu.SemaphoreType.DMA((1 + count,)),
            pltpu.SemaphoreType.DMA((count, hidden)),
        ],
        name="totals",
        **params(rows * width, 10 * rows * width),
    )(own, back, pltpu.with_memory_space_constraint(after, pltpu.HBM))


def in_grad_kernel(left_counts, right_counts, after_ref, *refs):
    del after_ref
    *refs, out_ref, scratch, sem = refs
    stores = []
    for n, at in enumerate(columns(out_ref.shape[1])):
        rest = list(refs)
        result = None
        for n_left, groups in zip(left_counts, right_counts):
            left = [rest.pop(0)[...] for _ in range(n_left)]
            right = []
            for count in groups:
                term = rest.pop(0)[:, at]
                for _ in range(count - 1):
                    term = term + rest.pop(0)[:, at]
                right.append(term)
            partial = lax.dot_general(
                jnp.concatenate(left, axis=0),
                jnp.concatenate(right, axis=0),
                (((0,), (0,)), ((), ())),
                preferred_element_type=F32,
            )
            partial = partial.astype(BF16).astype(F32)
            result = partial if result is None else result + partial
        scratch[:, at] = result.astype(BF16)
        stores.append(pltpu.make_async_copy(scratch.at[:, at], out_ref.at[:, at], sem.at[n]))
        stores[-1].start()
    for copy in stores:
        copy.wait()


def in_grad_of(after, *partials):
    operands = []
    for lefts, rights in partials:
        operands += lefts + [t for r in rights for t in r]
    rows, width = partials[0][0][0].shape[1], partials[0][1][0][0].shape[1]
    return pl.pallas_call(
        functools.partial(
            in_grad_kernel,
            [len(l) for l, _ in partials],
            [[len(t) for t in r] for _, r in partials],
        ),
        in_specs=[HBM] + [VMEM] * len(operands),
        out_specs=HBM,
        out_shape=jax.ShapeDtypeStruct((rows, width), BF16),
        scratch_shapes=[
            pltpu.VMEM((rows, width), BF16),
            pltpu.SemaphoreType.DMA((len(columns(width)),)),
        ],
        name="in_grad",
        **params(
            2 * sum(t.shape[0] for l, _ in partials for t in l) * rows * width,
            2 * sum(t.size for t in operands) + 2 * rows * width,
        ),
    )(pltpu.with_memory_space_constraint(after, pltpu.HBM), *in_vmem(*operands))


def local(activations, out_grad, gate_weight, up_weight, down_weight):
    n_blk, n_tensor = lax.axis_size("blk"), lax.axis_size("tensor")
    hidden = gate_weight.shape[2]
    step = -(-hidden // 8) * 8
    pairs = n_tensor == 2 and n_blk % 2 == 0
    w_gate, w_up, w_down = gate_weight[0].T, up_weight[0].T, down_weight[0]
    prev_down, prev_gate, prev_up = [from_behind(w, "blk", 1) for w in (w_down, w_gate, w_up)]
    weights = [prev_gate, prev_up]
    if pairs:
        axes = ("blk", "tensor")
        swap = [(0, 1), (1, 0)]
        on_chip = [(2 * b + j, 2 * (b + 1) + j) for b in range(0, n_blk, 2) for j in range(2)]
        across = [(2 * b + j, 2 * b + 1 - j) for b in range(0, n_blk, 2) for j in range(2)]
        other_gate, other_up = [lax.ppermute(w, "tensor", swap) for w in (w_gate, w_up)]

    w_gu, own_grads, own_hidden = own_meeting(activations, out_grad, w_gate, w_up, w_down, step)
    grad_hidden = grad_hidden_of(out_grad, prev_down, own_grads)
    early, late, prev_gu, *grads = second_meeting(
        activations,
        out_grad,
        grad_hidden,
        own_grads,
        weights,
        lax.axis_index("tensor"),
        2 if pairs else 1,
    )
    back_early, back_late = [from_behind(t, "blk", -1) for t in (early, late)]
    sums_early, sums_late = own_sums(activations, out_grad, own_hidden, own_grads, prev_gu)
    total_down, total_gate = totals(sums_early, back_early, 2, hidden, activations)
    if pairs:
        mine, sent = grads
        prev_other_even = lax.ppermute(prev_gu, axes, across)
        theirs = lax.ppermute(sent, "tensor", swap)
        other_gu = stack(other_gate, other_up, step, theirs)
        prev_other_odd = lax.ppermute(other_gu, axes, on_chip)
        in_grad = in_grad_of(
            total_gate,
            ([mine], [[w_gu], [prev_gu]]),
            ([theirs], [[other_gu], [prev_other_even, prev_other_odd]]),
        )
        after = in_grad
    else:
        after = in_grad_of(activations, (grads, [[w_gu], [prev_gu]]))
        in_grad = lax.psum_scatter(after, "tensor", scatter_dimension=0, tiled=True)
    [total_up] = totals(sums_late, back_late, 1, hidden, after)
    return (
        in_grad,
        total_gate.transpose(1, 2, 0),
        total_up.transpose(1, 2, 0),
        total_down.transpose(1, 0, 2),
    )


def solution(mesh):
    in_specs = (
        P("blk", None),
        P("blk", None),
        P("blk", None, "tensor"),
        P("blk", None, "tensor"),
        P("blk", "tensor", None),
    )
    out_specs = (
        P(("blk", "tensor"), None),
        P("blk", None, "tensor"),
        P("blk", None, "tensor"),
        P("blk", "tensor", None),
    )
    return jax.shard_map(local, mesh=mesh, in_specs=in_specs, out_specs=out_specs, check_vma=False)
```

```python
import functools

import jax
import jax.numpy as jnp
from jax import lax
from jax.experimental import pallas as pl
from jax.experimental.pallas import tpu as pltpu
from jax.sharding import PartitionSpec as P

F32 = jnp.float32
BF16 = jnp.bfloat16
VMEM_LIMIT = 16 * 2**20
VMEM = pl.BlockSpec(memory_space=pltpu.VMEM)
ANY = pl.BlockSpec(memory_space=pl.ANY)
HBM = pl.BlockSpec(memory_space=pltpu.HBM)
SMEM = pl.BlockSpec(memory_space=pltpu.SMEM)


def from_behind(value, axis, by):
    devices = lax.axis_size(axis)
    return lax.ppermute(value, axis, [(i, (i + by) % devices) for i in range(devices)])


def column_block(width, limit):
    block = limit
    while width % block:
        block -= 128
    return block


def columns(width, limit=1280):
    block = column_block(width, limit)
    return [pl.ds(at, block) for at in range(0, width, block)]


def in_vmem(*arrays):
    return [pltpu.with_memory_space_constraint(a, pltpu.VMEM) for a in arrays]


def params(flops, nbytes):
    return dict(
        compiler_params=pltpu.CompilerParams(vmem_limit_bytes=VMEM_LIMIT),
        cost_estimate=pl.CostEstimate(flops=flops, bytes_accessed=nbytes, transcendentals=0),
    )


def stacked(gate, up, step):
    if gate.shape[0] == step:
        return jnp.concatenate([gate, up], axis=0)
    pad = jnp.zeros((step - gate.shape[0], gate.shape[1]), gate.dtype)
    return jnp.concatenate([gate, pad, up, pad], axis=0)


def pre_of(stack_ref, gate_ref, up_ref, rows_ref):
    total = None
    for at in columns(stack_ref.shape[1]):
        weight = stacked(gate_ref[:, at], up_ref[:, at], stack_ref.shape[0] // 2)
        stack_ref[:, at] = weight
        term = lax.dot_general(
            weight, rows_ref[:, at], (((1,), (1,)), ((), ())), preferred_element_type=F32
        )
        total = term if total is None else total + term
    return total


def hidden_of(pre):
    step = pre.shape[0] // 2
    gate_pre, up_pre = pre[:step], pre[step:]
    return (gate_pre * jax.nn.sigmoid(gate_pre) * up_pre).astype(BF16)


def product(weight_ref, rows_ref):
    total = None
    for at in columns(weight_ref.shape[1]):
        term = lax.dot_general(
            weight_ref[:, at], rows_ref[:, at], (((1,), (1,)), ((), ())), preferred_element_type=F32
        )
        total = term if total is None else total + term
    return total


def grads_of(pre, grad_hidden):
    step, hidden = pre.shape[0] // 2, grad_hidden.shape[0]
    if step > hidden:
        pad = jnp.zeros((step - hidden, grad_hidden.shape[1]), F32)
        grad_hidden = jnp.concatenate([grad_hidden, pad], axis=0)
    gate_pre, up_pre = pre[:step], pre[step:]
    sigmoid_part = jax.nn.sigmoid(gate_pre)
    slope_part = sigmoid_part * (1.0 + gate_pre * (1.0 - sigmoid_part))
    grad_gate = (grad_hidden * up_pre * slope_part).astype(BF16)
    grad_up = (grad_hidden * (gate_pre * sigmoid_part)).astype(BF16)
    return jnp.concatenate([grad_gate, grad_up], axis=0)


def terms_of(early_ref, late_ref, hidden, grads, x_ref, g_ref):
    step = hidden.shape[0]
    for at in columns(x_ref.shape[1]):
        down = jnp.dot(hidden, g_ref[:, at], preferred_element_type=F32)
        gate_up = jnp.dot(grads, x_ref[:, at], preferred_element_type=F32)
        early = jnp.concatenate([down, gate_up[:step]], axis=0)
        early_ref[:, at] = early.astype(early_ref.dtype)
        late_ref[:, at] = gate_up[step:].astype(late_ref.dtype)


def own_kernel(x_ref, g_ref, gate_in, up_in, down_in, stack_ref, grads_ref, hidden_ref, gate_ref, up_ref, down_ref, sem):
    copies = [
        pltpu.make_async_copy(source, into, sem.at[n])
        for n, (source, into) in enumerate(
            [(gate_in, gate_ref), (up_in, up_ref), (down_in, down_ref)]
        )
    ]
    for copy in copies:
        copy.start()
    copies[0].wait()
    copies[1].wait()
    pre = pre_of(stack_ref, gate_ref, up_ref, x_ref)
    hidden_ref[...] = hidden_of(pre)
    copies[2].wait()
    grads_ref[...] = grads_of(pre, product(down_ref, g_ref))


def own_meeting(x, g, w_gate, w_up, w_down, step):
    rows, width = x.shape
    weights = [pltpu.with_memory_space_constraint(w, pltpu.HBM) for w in (w_gate, w_up, w_down)]
    return pl.pallas_call(
        own_kernel,
        in_specs=[VMEM] * 2 + [HBM] * 3,
        out_specs=[VMEM] * 3,
        out_shape=[
            pltpu.VMEM((2 * step, width), BF16),
            pltpu.VMEM((2 * step, rows), BF16),
            pltpu.VMEM((step, rows), BF16),
        ],
        scratch_shapes=[pltpu.VMEM(w_gate.shape, BF16)] * 3 + [pltpu.SemaphoreType.DMA((3,))],
        name="own_meeting",
        **params(6 * step * rows * width, 4 * rows * width),
    )(*in_vmem(x, g), *weights)


def grad_hidden_kernel(g_ref, down_ref, after_ref, out_ref):
    del after_ref
    out_ref[...] = product(down_ref, g_ref)


def grad_hidden_of(g, w_down, after):
    rows, width = g.shape
    return pl.pallas_call(
        grad_hidden_kernel,
        in_specs=[VMEM] * 2 + [ANY],
        out_specs=VMEM,
        out_shape=pltpu.VMEM((w_down.shape[0], rows), F32),
        name="grad_hidden",
        **params(2 * w_down.size * rows, 2 * g.size),
    )(*in_vmem(g, w_down), after)


def second_kernel(n_stacks, halves, x_ref, g_ref, prev_ref, own_ref, index_ref, *refs):
    weights, (early_ref, late_ref, *refs) = refs[: 2 * n_stacks], refs[2 * n_stacks :]
    stack_refs, grads_refs = refs[:n_stacks], refs[n_stacks:]
    step = late_ref.shape[0]
    pre = pre_of(stack_refs[0], weights[0], weights[1], x_ref)
    grads = grads_of(pre, prev_ref[...])
    terms_of(early_ref, late_ref, hidden_of(pre), grads, x_ref, g_ref)
    both = jnp.concatenate([own_ref[...], grads], axis=0)
    if halves == 1:
        grads_refs[0][...] = both
        return
    half = both.shape[1] // 2

    @pl.when(index_ref[0] == 0)
    def _():
        grads_refs[0][...] = both[:, :half]
        grads_refs[1][...] = both[:, half:]

    @pl.when(index_ref[0] != 0)
    def _():
        grads_refs[0][...] = both[:, half:]
        grads_refs[1][...] = both[:, :half]

    for n in range(1, n_stacks):
        for at in columns(x_ref.shape[1]):
            gate, up = weights[2 * n][:, at], weights[2 * n + 1][:, at]
            stack_refs[n][:, at] = stacked(gate, up, step)


def second_meeting(x, g, grad_hidden, own_grads, weights, index, halves):
    rows, width = x.shape
    step2 = own_grads.shape[0]
    n_stacks = len(weights) // 2
    return pl.pallas_call(
        functools.partial(second_kernel, n_stacks, halves),
        in_specs=[VMEM] * 4 + [SMEM] + [VMEM] * len(weights),
        out_specs=[VMEM] * (2 + n_stacks + halves),
        out_shape=[pltpu.VMEM((step2, width), BF16), pltpu.VMEM((step2 // 2, width), BF16)]
        + [pltpu.VMEM((step2, width), BF16)] * n_stacks
        + [pltpu.VMEM((2 * step2, rows // halves), BF16)] * halves,
        name="second_meeting",
        **params(6 * step2 * rows * width, 4 * rows * width),
    )(*in_vmem(x, g, grad_hidden, own_grads), index.reshape(1), *in_vmem(*weights))


def stack_kernel(gate_ref, up_ref, after_ref, out_ref):
    del after_ref
    for at in columns(out_ref.shape[1]):
        out_ref[:, at] = stacked(gate_ref[:, at], up_ref[:, at], out_ref.shape[0] // 2)


def stack(w_gate, w_up, step, after):
    width = w_gate.shape[1]
    return pl.pallas_call(
        stack_kernel,
        in_specs=[VMEM, VMEM, ANY],
        out_specs=VMEM,
        out_shape=pltpu.VMEM((2 * step, width), BF16),
        name="stack",
        **params(0, 8 * step * width),
    )(*in_vmem(w_gate, w_up), after)


def sums_kernel(x_ref, g_ref, hidden_ref, grads_ref, after_ref, early_ref, late_ref):
    del after_ref
    terms_of(early_ref, late_ref, hidden_ref[...], grads_ref[...], x_ref, g_ref)


def own_sums(x, g, hidden, grads, after):
    rows, width = x.shape
    return pl.pallas_call(
        sums_kernel,
        in_specs=[VMEM] * 4 + [ANY],
        out_specs=[VMEM] * 2,
        out_shape=[pltpu.VMEM((n * hidden.shape[0], width), F32) for n in (2, 1)],
        name="own_sums",
        **params(6 * hidden.shape[0] * rows * width, 4 * rows * width),
    )(*in_vmem(x, g, hidden, grads), after)


def total_kernel(own_ref, back_ref, after_ref, *refs):
    del after_ref
    out_refs, (total_ref, sem) = refs[:-2], refs[-2:]
    step, hidden = own_ref.shape[0] // len(out_refs), out_refs[0].shape[0]
    stores = []
    for k, out_ref in enumerate(out_refs):
        for first in range(0, step, 8):
            part = pl.ds(k * step + first, 8)
            total_ref[part, :] = own_ref[part, :] + back_ref[part, :].astype(F32)
            for r in range(first, min(first + 8, hidden)):
                row = total_ref.at[pl.ds(k * step + r, 1), :]
                stores.append(pltpu.make_async_copy(row, out_ref.at[r], sem.at[k, r]))
                stores[-1].start()
    for copy in stores:
        copy.wait()


def totals(own, back, count, hidden, after, place=HBM):
    rows, width = own.shape
    return pl.pallas_call(
        total_kernel,
        in_specs=[VMEM, VMEM, place],
        out_specs=[HBM] * count,
        out_shape=[jax.ShapeDtypeStruct((hidden, 1, width), F32)] * count,
        scratch_shapes=[
            pltpu.VMEM((rows, width), F32),
            pltpu.SemaphoreType.DMA((count, hidden)),
        ],
        name="totals",
        **params(rows * width, 10 * rows * width),
    )(*in_vmem(own, back), pltpu.with_memory_space_constraint(after, pltpu.HBM) if place is HBM else after)


def in_grad_kernel(left_counts, right_counts, after_ref, *refs):
    del after_ref
    *refs, out_ref, scratch, sem = refs
    stores = []
    for n, at in enumerate(columns(out_ref.shape[1])):
        rest = list(refs)
        result = None
        for n_left, groups in zip(left_counts, right_counts):
            left = [rest.pop(0)[...] for _ in range(n_left)]
            right = []
            for count in groups:
                term = rest.pop(0)[:, at]
                for _ in range(count - 1):
                    term = term + rest.pop(0)[:, at]
                right.append(term)
            partial = lax.dot_general(
                jnp.concatenate(left, axis=0),
                jnp.concatenate(right, axis=0),
                (((0,), (0,)), ((), ())),
                preferred_element_type=F32,
            )
            partial = partial.astype(BF16).astype(F32)
            result = partial if result is None else result + partial
        scratch[:, at] = result.astype(BF16)
        stores.append(pltpu.make_async_copy(scratch.at[:, at], out_ref.at[:, at], sem.at[n]))
        stores[-1].start()
    for copy in stores:
        copy.wait()


def in_grad_of(after, *partials):
    operands = []
    for lefts, rights in partials:
        operands += lefts + [t for r in rights for t in r]
    rows, width = partials[0][0][0].shape[1], partials[0][1][0][0].shape[1]
    return pl.pallas_call(
        functools.partial(
            in_grad_kernel,
            [len(l) for l, _ in partials],
            [[len(t) for t in r] for _, r in partials],
        ),
        in_specs=[HBM] + [VMEM] * len(operands),
        out_specs=HBM,
        out_shape=jax.ShapeDtypeStruct((rows, width), BF16),
        scratch_shapes=[
            pltpu.VMEM((rows, width), BF16),
            pltpu.SemaphoreType.DMA((len(columns(width)),)),
        ],
        name="in_grad",
        **params(
            2 * sum(t.shape[0] for l, _ in partials for t in l) * rows * width,
            2 * sum(t.size for t in operands) + 2 * rows * width,
        ),
    )(pltpu.with_memory_space_constraint(after, pltpu.HBM), *in_vmem(*operands))


def dot_left(left, right):
    return lax.dot_general(left, right, (((0,), (0,)), ((), ())), preferred_element_type=F32)


def ready_part_kernel(mine_ref, own_ref, prev_ref, theirs_ref, other_ref, after_ref, mine_out, theirs_out, done_ref):
    del after_ref
    step2 = other_ref.shape[0]
    done_ref[...] = jnp.zeros_like(done_ref)
    for at in columns(own_ref.shape[1]):
        both = jnp.concatenate([own_ref[:, at], prev_ref[:, at]], axis=0)
        mine_out[:, at] = dot_left(mine_ref[...], both).astype(BF16)
        theirs_out[:, at] = dot_left(theirs_ref[:step2, :], other_ref[:, at])


def ready_part(mine, own, prev, theirs, other, after):
    rows, width = mine.shape[1], own.shape[1]
    return pl.pallas_call(
        ready_part_kernel,
        in_specs=[VMEM] * 5 + [ANY],
        out_specs=[VMEM] * 3,
        out_shape=[
            pltpu.VMEM((rows, width), BF16),
            pltpu.VMEM((rows, width), F32),
            pltpu.VMEM((8, 128), F32),
        ],
        name="ready_part",
        **params(6 * other.shape[0] * rows * width, 6 * rows * width),
    )(*in_vmem(mine, own, prev, theirs, other), after)


def last_part_kernel(mine_ref, part_ref, theirs_ref, even_ref, odd_ref, after_ref, out_ref, scratch, sem):
    del after_ref
    stores = []
    for n, at in enumerate(columns(out_ref.shape[1])):
        term = dot_left(theirs_ref[even_ref.shape[0] :, :], even_ref[:, at] + odd_ref[:, at])
        theirs = (part_ref[:, at] + term).astype(BF16)
        scratch[:, at] = (mine_ref[:, at].astype(F32) + theirs.astype(F32)).astype(BF16)
        stores.append(pltpu.make_async_copy(scratch.at[:, at], out_ref.at[:, at], sem.at[n]))
        stores[-1].start()
    for copy in stores:
        copy.wait()


def last_part(mine_partial, part, theirs, even, odd, after):
    rows, width = part.shape
    return pl.pallas_call(
        last_part_kernel,
        in_specs=[VMEM] * 5 + [HBM],
        out_specs=HBM,
        out_shape=jax.ShapeDtypeStruct((rows, width), BF16),
        scratch_shapes=[
            pltpu.VMEM((rows, width), BF16),
            pltpu.SemaphoreType.DMA((len(columns(width)),)),
        ],
        name="last_part",
        **params(2 * even.shape[0] * rows * width, 8 * rows * width),
    )(
        *in_vmem(mine_partial, part, theirs, even, odd),
        pltpu.with_memory_space_constraint(after, pltpu.HBM),
    )


def local(activations, out_grad, gate_weight, up_weight, down_weight):
    n_blk, n_tensor = lax.axis_size("blk"), lax.axis_size("tensor")
    hidden = gate_weight.shape[2]
    step = -(-hidden // 8) * 8
    pairs = n_tensor == 2 and n_blk % 2 == 0
    w_gate, w_up, w_down = gate_weight[0].T, up_weight[0].T, down_weight[0]
    prev_down, prev_gate, prev_up = [from_behind(w, "blk", 1) for w in (w_down, w_gate, w_up)]
    weights = [prev_gate, prev_up]
    if pairs:
        axes = ("blk", "tensor")
        swap = [(0, 1), (1, 0)]
        on_chip = [(2 * b + j, 2 * (b + 1) + j) for b in range(0, n_blk, 2) for j in range(2)]
        across = [(2 * b + j, 2 * b + 1 - j) for b in range(0, n_blk, 2) for j in range(2)]
        other_gate, other_up = [lax.ppermute(w, "tensor", swap) for w in (w_gate, w_up)]

    w_gu, own_grads, own_hidden = own_meeting(activations, out_grad, w_gate, w_up, w_down, step)
    grad_hidden = grad_hidden_of(out_grad, prev_down, own_grads)
    early, late, prev_gu, *grads = second_meeting(
        activations,
        out_grad,
        grad_hidden,
        own_grads,
        weights,
        lax.axis_index("tensor"),
        2 if pairs else 1,
    )
    back_early, back_late = [from_behind(t, "blk", -1) for t in (early, late)]
    sums_early, sums_late = own_sums(activations, out_grad, own_hidden, own_grads, back_early)
    if pairs:
        mine, sent = grads
        prev_other_even = lax.ppermute(prev_gu, axes, across)
        theirs = lax.ppermute(sent, "tensor", swap)
        other_gu = stack(other_gate, other_up, step, theirs)
        prev_other_odd = lax.ppermute(other_gu, axes, on_chip)
        mine_partial, part, done = ready_part(mine, w_gu, prev_gu, theirs, other_gu, sent)
    else:
        done = prev_gu
    total_down, total_gate = totals(sums_early, back_early, 2, hidden, activations)
    if pairs:
        after = in_grad = last_part(
            mine_partial, part, theirs, prev_other_even, prev_other_odd, total_gate
        )
    else:
        after = in_grad_of(activations, (grads, [[w_gu], [prev_gu]]))
        in_grad = lax.psum_scatter(after, "tensor", scatter_dimension=0, tiled=True)
    [total_up] = totals(sums_late, back_late, 1, hidden, after)
    return (
        in_grad,
        total_gate.transpose(1, 2, 0),
        total_up.transpose(1, 2, 0),
        total_down.transpose(1, 0, 2),
    )


def solution(mesh):
    in_specs = (
        P("blk", None),
        P("blk", None),
        P("blk", None, "tensor"),
        P("blk", None, "tensor"),
        P("blk", "tensor", None),
    )
    out_specs = (
        P(("blk", "tensor"), None),
        P("blk", None, "tensor"),
        P("blk", None, "tensor"),
        P("blk", "tensor", None),
    )
    return jax.shard_map(local, mesh=mesh, in_specs=in_specs, out_specs=out_specs, check_vma=False)
```

```python
import functools

import jax
import jax.numpy as jnp
from jax import lax
from jax.experimental import pallas as pl
from jax.experimental.pallas import tpu as pltpu
from jax.sharding import PartitionSpec as P

F32 = jnp.float32
BF16 = jnp.bfloat16
VMEM_LIMIT = 16 * 2**20
VMEM = pl.BlockSpec(memory_space=pltpu.VMEM)
ANY = pl.BlockSpec(memory_space=pl.ANY)
HBM = pl.BlockSpec(memory_space=pltpu.HBM)
SMEM = pl.BlockSpec(memory_space=pltpu.SMEM)


def from_behind(value, axis, by):
    devices = lax.axis_size(axis)
    return lax.ppermute(value, axis, [(i, (i + by) % devices) for i in range(devices)])


def column_block(width, limit):
    block = limit
    while width % block:
        block -= 128
    return block


def columns(width, limit=1280):
    block = column_block(width, limit)
    return [pl.ds(at, block) for at in range(0, width, block)]


def in_vmem(*arrays):
    return [pltpu.with_memory_space_constraint(a, pltpu.VMEM) for a in arrays]


def params(flops, nbytes):
    return dict(
        compiler_params=pltpu.CompilerParams(vmem_limit_bytes=VMEM_LIMIT),
        cost_estimate=pl.CostEstimate(flops=flops, bytes_accessed=nbytes, transcendentals=0),
    )


def stacked(gate, up, step):
    if gate.shape[0] == step:
        return jnp.concatenate([gate, up], axis=0)
    pad = jnp.zeros((step - gate.shape[0], gate.shape[1]), gate.dtype)
    return jnp.concatenate([gate, pad, up, pad], axis=0)


def pre_of(stack_ref, gate_ref, up_ref, rows_ref):
    total = None
    for at in columns(stack_ref.shape[1]):
        weight = stacked(gate_ref[:, at], up_ref[:, at], stack_ref.shape[0] // 2)
        stack_ref[:, at] = weight
        term = lax.dot_general(
            weight, rows_ref[:, at], (((1,), (1,)), ((), ())), preferred_element_type=F32
        )
        total = term if total is None else total + term
    return total


def hidden_of(pre):
    step = pre.shape[0] // 2
    gate_pre, up_pre = pre[:step], pre[step:]
    return (gate_pre * jax.nn.sigmoid(gate_pre) * up_pre).astype(BF16)


def product(weight_ref, rows_ref):
    total = None
    for at in columns(weight_ref.shape[1]):
        term = lax.dot_general(
            weight_ref[:, at], rows_ref[:, at], (((1,), (1,)), ((), ())), preferred_element_type=F32
        )
        total = term if total is None else total + term
    return total


def grads_of(pre, grad_hidden):
    step, hidden = pre.shape[0] // 2, grad_hidden.shape[0]
    if step > hidden:
        pad = jnp.zeros((step - hidden, grad_hidden.shape[1]), F32)
        grad_hidden = jnp.concatenate([grad_hidden, pad], axis=0)
    gate_pre, up_pre = pre[:step], pre[step:]
    sigmoid_part = jax.nn.sigmoid(gate_pre)
    slope_part = sigmoid_part * (1.0 + gate_pre * (1.0 - sigmoid_part))
    grad_gate = (grad_hidden * up_pre * slope_part).astype(BF16)
    grad_up = (grad_hidden * (gate_pre * sigmoid_part)).astype(BF16)
    return jnp.concatenate([grad_gate, grad_up], axis=0)


def terms_of(early_ref, late_ref, hidden, grads, x_ref, g_ref):
    step = hidden.shape[0]
    for at in columns(x_ref.shape[1]):
        down = jnp.dot(hidden, g_ref[:, at], preferred_element_type=F32)
        gate_up = jnp.dot(grads, x_ref[:, at], preferred_element_type=F32)
        early = jnp.concatenate([down, gate_up[:step]], axis=0)
        early_ref[:, at] = early.astype(early_ref.dtype)
        late_ref[:, at] = gate_up[step:].astype(late_ref.dtype)


def own_kernel(x_ref, g_ref, gate_in, up_in, down_in, stack_ref, grads_ref, hidden_ref, gate_ref, up_ref, down_ref, sem):
    copies = [
        pltpu.make_async_copy(source, into, sem.at[n])
        for n, (source, into) in enumerate(
            [(gate_in, gate_ref), (up_in, up_ref), (down_in, down_ref)]
        )
    ]
    for copy in copies:
        copy.start()
    copies[0].wait()
    copies[1].wait()
    pre = pre_of(stack_ref, gate_ref, up_ref, x_ref)
    hidden_ref[...] = hidden_of(pre)
    copies[2].wait()
    grads_ref[...] = grads_of(pre, product(down_ref, g_ref))


def own_meeting(x, g, w_gate, w_up, w_down, step):
    rows, width = x.shape
    weights = [pltpu.with_memory_space_constraint(w, pltpu.HBM) for w in (w_gate, w_up, w_down)]
    return pl.pallas_call(
        own_kernel,
        in_specs=[VMEM] * 2 + [HBM] * 3,
        out_specs=[VMEM] * 3,
        out_shape=[
            pltpu.VMEM((2 * step, width), BF16),
            pltpu.VMEM((2 * step, rows), BF16),
            pltpu.VMEM((step, rows), BF16),
        ],
        scratch_shapes=[pltpu.VMEM(w_gate.shape, BF16)] * 3 + [pltpu.SemaphoreType.DMA((3,))],
        name="own_meeting",
        **params(6 * step * rows * width, 4 * rows * width),
    )(*in_vmem(x, g), *weights)


def grad_hidden_kernel(g_ref, down_ref, after_ref, out_ref):
    del after_ref
    out_ref[...] = product(down_ref, g_ref)


def grad_hidden_of(g, w_down, after):
    rows, width = g.shape
    return pl.pallas_call(
        grad_hidden_kernel,
        in_specs=[VMEM] * 2 + [ANY],
        out_specs=VMEM,
        out_shape=pltpu.VMEM((w_down.shape[0], rows), F32),
        name="grad_hidden",
        **params(2 * w_down.size * rows, 2 * g.size),
    )(*in_vmem(g, w_down), after)


def second_kernel(n_stacks, halves, x_ref, g_ref, prev_ref, own_ref, index_ref, *refs):
    weights, (early_ref, late_ref, *refs) = refs[: 2 * n_stacks], refs[2 * n_stacks :]
    stack_refs, grads_refs = refs[:n_stacks], refs[n_stacks:]
    step = late_ref.shape[0]
    pre = pre_of(stack_refs[0], weights[0], weights[1], x_ref)
    grads = grads_of(pre, prev_ref[...])
    terms_of(early_ref, late_ref, hidden_of(pre), grads, x_ref, g_ref)
    both = jnp.concatenate([own_ref[...], grads], axis=0)
    if halves == 1:
        grads_refs[0][...] = both
        return
    half = both.shape[1] // 2

    @pl.when(index_ref[0] == 0)
    def _():
        grads_refs[0][...] = both[:, :half]
        grads_refs[1][...] = both[:, half:]

    @pl.when(index_ref[0] != 0)
    def _():
        grads_refs[0][...] = both[:, half:]
        grads_refs[1][...] = both[:, :half]

    for n in range(1, n_stacks):
        for at in columns(x_ref.shape[1]):
            gate, up = weights[2 * n][:, at], weights[2 * n + 1][:, at]
            stack_refs[n][:, at] = stacked(gate, up, step)


def second_meeting(x, g, grad_hidden, own_grads, weights, index, halves):
    rows, width = x.shape
    step2 = own_grads.shape[0]
    n_stacks = len(weights) // 2
    return pl.pallas_call(
        functools.partial(second_kernel, n_stacks, halves),
        in_specs=[VMEM] * 4 + [SMEM] + [VMEM] * len(weights),
        out_specs=[VMEM] * (2 + n_stacks + halves),
        out_shape=[pltpu.VMEM((step2, width), BF16), pltpu.VMEM((step2 // 2, width), BF16)]
        + [pltpu.VMEM((step2, width), BF16)] * n_stacks
        + [pltpu.VMEM((2 * step2, rows // halves), BF16)] * halves,
        name="second_meeting",
        **params(6 * step2 * rows * width, 4 * rows * width),
    )(*in_vmem(x, g, grad_hidden, own_grads), index.reshape(1), *in_vmem(*weights))


def stack_kernel(gate_ref, up_ref, after_ref, out_ref):
    del after_ref
    for at in columns(out_ref.shape[1]):
        out_ref[:, at] = stacked(gate_ref[:, at], up_ref[:, at], out_ref.shape[0] // 2)


def stack(w_gate, w_up, step, after):
    width = w_gate.shape[1]
    return pl.pallas_call(
        stack_kernel,
        in_specs=[VMEM, VMEM, ANY],
        out_specs=VMEM,
        out_shape=pltpu.VMEM((2 * step, width), BF16),
        name="stack",
        **params(0, 8 * step * width),
    )(*in_vmem(w_gate, w_up), after)


def sums_kernel(x_ref, g_ref, hidden_ref, grads_ref, after_ref, early_ref, late_ref):
    del after_ref
    terms_of(early_ref, late_ref, hidden_ref[...], grads_ref[...], x_ref, g_ref)


def own_sums(x, g, hidden, grads, after):
    rows, width = x.shape
    return pl.pallas_call(
        sums_kernel,
        in_specs=[VMEM] * 4 + [ANY],
        out_specs=[VMEM] * 2,
        out_shape=[pltpu.VMEM((n * hidden.shape[0], width), F32) for n in (2, 1)],
        name="own_sums",
        **params(6 * hidden.shape[0] * rows * width, 4 * rows * width),
    )(*in_vmem(x, g, hidden, grads), after)


def total_kernel(own_ref, back_ref, after_ref, *refs):
    del after_ref
    out_refs, (total_ref, sem) = refs[:-2], refs[-2:]
    step, hidden = own_ref.shape[0] // len(out_refs), out_refs[0].shape[0]
    stores = []
    for k, out_ref in enumerate(out_refs):
        for first in range(0, step, 8):
            part = pl.ds(k * step + first, 8)
            total_ref[part, :] = own_ref[part, :] + back_ref[part, :].astype(F32)
            for r in range(first, min(first + 8, hidden)):
                row = total_ref.at[pl.ds(k * step + r, 1), :]
                stores.append(pltpu.make_async_copy(row, out_ref.at[r], sem.at[k, r]))
                stores[-1].start()
    for copy in stores:
        copy.wait()


def totals(own, back, count, hidden, after, place=HBM):
    rows, width = own.shape
    return pl.pallas_call(
        total_kernel,
        in_specs=[VMEM, VMEM, place],
        out_specs=[HBM] * count,
        out_shape=[jax.ShapeDtypeStruct((hidden, 1, width), F32)] * count,
        scratch_shapes=[
            pltpu.VMEM((rows, width), F32),
            pltpu.SemaphoreType.DMA((count, hidden)),
        ],
        name="totals",
        **params(rows * width, 10 * rows * width),
    )(*in_vmem(own, back), pltpu.with_memory_space_constraint(after, pltpu.HBM) if place is HBM else after)


def in_grad_kernel(left_counts, right_counts, after_ref, *refs):
    del after_ref
    *refs, out_ref, scratch, sem = refs
    stores = []
    for n, at in enumerate(columns(out_ref.shape[1])):
        rest = list(refs)
        result = None
        for n_left, groups in zip(left_counts, right_counts):
            left = [rest.pop(0)[...] for _ in range(n_left)]
            right = []
            for count in groups:
                term = rest.pop(0)[:, at]
                for _ in range(count - 1):
                    term = term + rest.pop(0)[:, at]
                right.append(term)
            partial = lax.dot_general(
                jnp.concatenate(left, axis=0),
                jnp.concatenate(right, axis=0),
                (((0,), (0,)), ((), ())),
                preferred_element_type=F32,
            )
            partial = partial.astype(BF16).astype(F32)
            result = partial if result is None else result + partial
        scratch[:, at] = result.astype(BF16)
        stores.append(pltpu.make_async_copy(scratch.at[:, at], out_ref.at[:, at], sem.at[n]))
        stores[-1].start()
    for copy in stores:
        copy.wait()


def in_grad_of(after, *partials):
    operands = []
    for lefts, rights in partials:
        operands += lefts + [t for r in rights for t in r]
    rows, width = partials[0][0][0].shape[1], partials[0][1][0][0].shape[1]
    return pl.pallas_call(
        functools.partial(
            in_grad_kernel,
            [len(l) for l, _ in partials],
            [[len(t) for t in r] for _, r in partials],
        ),
        in_specs=[HBM] + [VMEM] * len(operands),
        out_specs=HBM,
        out_shape=jax.ShapeDtypeStruct((rows, width), BF16),
        scratch_shapes=[
            pltpu.VMEM((rows, width), BF16),
            pltpu.SemaphoreType.DMA((len(columns(width)),)),
        ],
        name="in_grad",
        **params(
            2 * sum(t.shape[0] for l, _ in partials for t in l) * rows * width,
            2 * sum(t.size for t in operands) + 2 * rows * width,
        ),
    )(pltpu.with_memory_space_constraint(after, pltpu.HBM), *in_vmem(*operands))


def dot_left(left, right):
    return lax.dot_general(left, right, (((0,), (0,)), ((), ())), preferred_element_type=F32)


def ready_part_kernel(mine_ref, own_ref, prev_ref, theirs_ref, other_ref, after_ref, mine_out, theirs_out, done_ref):
    del after_ref
    step2 = other_ref.shape[0]
    done_ref[...] = jnp.zeros_like(done_ref)
    for at in columns(own_ref.shape[1]):
        both = jnp.concatenate([own_ref[:, at], prev_ref[:, at]], axis=0)
        mine_out[:, at] = dot_left(mine_ref[...], both).astype(BF16)
        theirs_out[:, at] = dot_left(theirs_ref[:step2, :], other_ref[:, at])


def ready_part(mine, own, prev, theirs, other, after):
    rows, width = mine.shape[1], own.shape[1]
    return pl.pallas_call(
        ready_part_kernel,
        in_specs=[VMEM] * 5 + [ANY],
        out_specs=[VMEM] * 3,
        out_shape=[
            pltpu.VMEM((rows, width), BF16),
            pltpu.VMEM((rows, width), F32),
            pltpu.VMEM((8, 128), F32),
        ],
        name="ready_part",
        **params(6 * other.shape[0] * rows * width, 6 * rows * width),
    )(*in_vmem(mine, own, prev, theirs, other), after)


def add_rows(total_ref, own_ref, back_ref, first_row, out_ref, sem):
    hidden, stores = out_ref.shape[0], []
    for first in range(0, hidden, 8):
        part = pl.ds(first_row + first, 8)
        total_ref[part, :] = own_ref[part, :] + back_ref[part, :].astype(F32)
        for r in range(first, min(first + 8, hidden)):
            row = total_ref.at[pl.ds(first_row + r, 1), :]
            stores.append(pltpu.make_async_copy(row, out_ref.at[r], sem.at[r]))
            stores[-1].start()
    return stores


def last_kernel(mine_ref, part_ref, theirs_ref, even_ref, odd_ref, own_ref, back_ref, after_ref, out_ref, up_ref, scratch, total_ref, sem, up_sem):
    del after_ref
    stores = add_rows(total_ref, own_ref, back_ref, 0, up_ref, up_sem)
    for n, at in enumerate(columns(out_ref.shape[1])):
        term = dot_left(theirs_ref[even_ref.shape[0] :, :], even_ref[:, at] + odd_ref[:, at])
        theirs = (part_ref[:, at] + term).astype(BF16)
        scratch[:, at] = (mine_ref[:, at].astype(F32) + theirs.astype(F32)).astype(BF16)
        stores.append(pltpu.make_async_copy(scratch.at[:, at], out_ref.at[:, at], sem.at[n]))
        stores[-1].start()
    for copy in stores:
        copy.wait()


def last_part(mine_partial, part, theirs, even, odd, own, back, hidden, after):
    rows, width = part.shape
    return pl.pallas_call(
        last_kernel,
        in_specs=[VMEM] * 7 + [HBM],
        out_specs=[HBM] * 2,
        out_shape=[
            jax.ShapeDtypeStruct((rows, width), BF16),
            jax.ShapeDtypeStruct((hidden, 1, width), F32),
        ],
        scratch_shapes=[
            pltpu.VMEM((rows, width), BF16),
            pltpu.VMEM(own.shape, F32),
            pltpu.SemaphoreType.DMA((len(columns(width)),)),
            pltpu.SemaphoreType.DMA((hidden,)),
        ],
        name="last_part",
        **params(2 * even.shape[0] * rows * width, 8 * rows * width),
    )(
        *in_vmem(mine_partial, part, theirs, even, odd, own, back),
        pltpu.with_memory_space_constraint(after, pltpu.HBM),
    )


def local(activations, out_grad, gate_weight, up_weight, down_weight):
    n_blk, n_tensor = lax.axis_size("blk"), lax.axis_size("tensor")
    hidden = gate_weight.shape[2]
    step = -(-hidden // 8) * 8
    pairs = n_tensor == 2 and n_blk % 2 == 0
    w_gate, w_up, w_down = gate_weight[0].T, up_weight[0].T, down_weight[0]
    prev_down, prev_gate, prev_up = [from_behind(w, "blk", 1) for w in (w_down, w_gate, w_up)]
    weights = [prev_gate, prev_up]
    if pairs:
        axes = ("blk", "tensor")
        swap = [(0, 1), (1, 0)]
        on_chip = [(2 * b + j, 2 * (b + 1) + j) for b in range(0, n_blk, 2) for j in range(2)]
        across = [(2 * b + j, 2 * b + 1 - j) for b in range(0, n_blk, 2) for j in range(2)]
        other_gate, other_up = [lax.ppermute(w, "tensor", swap) for w in (w_gate, w_up)]

    w_gu, own_grads, own_hidden = own_meeting(activations, out_grad, w_gate, w_up, w_down, step)
    grad_hidden = grad_hidden_of(out_grad, prev_down, own_grads)
    early, late, prev_gu, *grads = second_meeting(
        activations,
        out_grad,
        grad_hidden,
        own_grads,
        weights,
        lax.axis_index("tensor"),
        2 if pairs else 1,
    )
    back_early, back_late = [from_behind(t, "blk", -1) for t in (early, late)]
    sums_early, sums_late = own_sums(activations, out_grad, own_hidden, own_grads, back_early)
    if pairs:
        mine, sent = grads
        prev_other_even = lax.ppermute(prev_gu, axes, across)
        theirs = lax.ppermute(sent, "tensor", swap)
        other_gu = stack(other_gate, other_up, step, theirs)
        prev_other_odd = lax.ppermute(other_gu, axes, on_chip)
        mine_partial, part, done = ready_part(mine, w_gu, prev_gu, theirs, other_gu, sums_late)
    else:
        done = prev_gu
    total_down, total_gate = totals(sums_early, back_early, 2, hidden, activations)
    if pairs:
        in_grad, total_up = last_part(
            mine_partial,
            part,
            theirs,
            prev_other_even,
            prev_other_odd,
            sums_late,
            back_late,
            hidden,
            total_gate,
        )
    else:
        after = in_grad_of(activations, (grads, [[w_gu], [prev_gu]]))
        in_grad = lax.psum_scatter(after, "tensor", scatter_dimension=0, tiled=True)
        [total_up] = totals(sums_late, back_late, 1, hidden, after)
    return (
        in_grad,
        total_gate.transpose(1, 2, 0),
        total_up.transpose(1, 2, 0),
        total_down.transpose(1, 0, 2),
    )


def solution(mesh):
    in_specs = (
        P("blk", None),
        P("blk", None),
        P("blk", None, "tensor"),
        P("blk", None, "tensor"),
        P("blk", "tensor", None),
    )
    out_specs = (
        P(("blk", "tensor"), None),
        P("blk", None, "tensor"),
        P("blk", None, "tensor"),
        P("blk", "tensor", None),
    )
    return jax.shard_map(local, mesh=mesh, in_specs=in_specs, out_specs=out_specs, check_vma=False)
```

```python
import functools

import jax
import jax.numpy as jnp
from jax import lax
from jax.experimental import pallas as pl
from jax.experimental.pallas import tpu as pltpu
from jax.sharding import PartitionSpec as P

F32 = jnp.float32
BF16 = jnp.bfloat16
VMEM_LIMIT = 16 * 2**20
VMEM = pl.BlockSpec(memory_space=pltpu.VMEM)
ANY = pl.BlockSpec(memory_space=pl.ANY)
HBM = pl.BlockSpec(memory_space=pltpu.HBM)
SMEM = pl.BlockSpec(memory_space=pltpu.SMEM)


def from_behind(value, axis, by):
    devices = lax.axis_size(axis)
    return lax.ppermute(value, axis, [(i, (i + by) % devices) for i in range(devices)])


def column_block(width, limit):
    block = limit
    while width % block:
        block -= 128
    return block


def columns(width, limit=1280):
    block = column_block(width, limit)
    return [pl.ds(at, block) for at in range(0, width, block)]


def in_vmem(*arrays):
    return [pltpu.with_memory_space_constraint(a, pltpu.VMEM) for a in arrays]


def params(flops, nbytes):
    return dict(
        compiler_params=pltpu.CompilerParams(vmem_limit_bytes=VMEM_LIMIT),
        cost_estimate=pl.CostEstimate(flops=flops, bytes_accessed=nbytes, transcendentals=0),
    )


def stacked(gate, up, step):
    if gate.shape[0] == step:
        return jnp.concatenate([gate, up], axis=0)
    pad = jnp.zeros((step - gate.shape[0], gate.shape[1]), gate.dtype)
    return jnp.concatenate([gate, pad, up, pad], axis=0)


def pre_of(stack_ref, gate_ref, up_ref, rows_ref):
    total = None
    for at in columns(stack_ref.shape[1]):
        weight = stacked(gate_ref[:, at], up_ref[:, at], stack_ref.shape[0] // 2)
        stack_ref[:, at] = weight
        term = lax.dot_general(
            weight, rows_ref[:, at], (((1,), (1,)), ((), ())), preferred_element_type=F32
        )
        total = term if total is None else total + term
    return total


def hidden_of(pre):
    step = pre.shape[0] // 2
    gate_pre, up_pre = pre[:step], pre[step:]
    return (gate_pre * jax.nn.sigmoid(gate_pre) * up_pre).astype(BF16)


def product(weight_ref, rows_ref):
    total = None
    for at in columns(weight_ref.shape[1]):
        term = lax.dot_general(
            weight_ref[:, at], rows_ref[:, at], (((1,), (1,)), ((), ())), preferred_element_type=F32
        )
        total = term if total is None else total + term
    return total


def grads_of(pre, grad_hidden):
    step, hidden = pre.shape[0] // 2, grad_hidden.shape[0]
    if step > hidden:
        pad = jnp.zeros((step - hidden, grad_hidden.shape[1]), F32)
        grad_hidden = jnp.concatenate([grad_hidden, pad], axis=0)
    gate_pre, up_pre = pre[:step], pre[step:]
    sigmoid_part = jax.nn.sigmoid(gate_pre)
    slope_part = sigmoid_part * (1.0 + gate_pre * (1.0 - sigmoid_part))
    grad_gate = (grad_hidden * up_pre * slope_part).astype(BF16)
    grad_up = (grad_hidden * (gate_pre * sigmoid_part)).astype(BF16)
    return jnp.concatenate([grad_gate, grad_up], axis=0)


def terms_of(early_ref, late_ref, hidden, grads, x_ref, g_ref):
    step = hidden.shape[0]
    for at in columns(x_ref.shape[1]):
        down = jnp.dot(hidden, g_ref[:, at], preferred_element_type=F32)
        gate_up = jnp.dot(grads, x_ref[:, at], preferred_element_type=F32)
        early = jnp.concatenate([down, gate_up[:step]], axis=0)
        early_ref[:, at] = early.astype(early_ref.dtype)
        late_ref[:, at] = gate_up[step:].astype(late_ref.dtype)


def own_kernel(x_ref, g_ref, gate_in, up_in, down_in, stack_ref, grads_ref, hidden_ref, gate_ref, up_ref, down_ref, sem):
    copies = [
        pltpu.make_async_copy(source, into, sem.at[n])
        for n, (source, into) in enumerate(
            [(gate_in, gate_ref), (up_in, up_ref), (down_in, down_ref)]
        )
    ]
    for copy in copies:
        copy.start()
    copies[0].wait()
    copies[1].wait()
    pre = pre_of(stack_ref, gate_ref, up_ref, x_ref)
    hidden_ref[...] = hidden_of(pre)
    copies[2].wait()
    grads_ref[...] = grads_of(pre, product(down_ref, g_ref))


def own_meeting(x, g, w_gate, w_up, w_down, step):
    rows, width = x.shape
    weights = [pltpu.with_memory_space_constraint(w, pltpu.HBM) for w in (w_gate, w_up, w_down)]
    return pl.pallas_call(
        own_kernel,
        in_specs=[VMEM] * 2 + [HBM] * 3,
        out_specs=[VMEM] * 3,
        out_shape=[
            pltpu.VMEM((2 * step, width), BF16),
            pltpu.VMEM((2 * step, rows), BF16),
            pltpu.VMEM((step, rows), BF16),
        ],
        scratch_shapes=[pltpu.VMEM(w_gate.shape, BF16)] * 3 + [pltpu.SemaphoreType.DMA((3,))],
        name="own_meeting",
        **params(6 * step * rows * width, 4 * rows * width),
    )(*in_vmem(x, g), *weights)


def grad_hidden_kernel(g_ref, down_ref, after_ref, out_ref):
    del after_ref
    out_ref[...] = product(down_ref, g_ref)


def grad_hidden_of(g, w_down, after):
    rows, width = g.shape
    return pl.pallas_call(
        grad_hidden_kernel,
        in_specs=[VMEM] * 2 + [ANY],
        out_specs=VMEM,
        out_shape=pltpu.VMEM((w_down.shape[0], rows), F32),
        name="grad_hidden",
        **params(2 * w_down.size * rows, 2 * g.size),
    )(*in_vmem(g, w_down), after)


def second_kernel(n_stacks, halves, x_ref, g_ref, prev_ref, own_ref, index_ref, *refs):
    weights, (early_ref, late_ref, *refs) = refs[: 2 * n_stacks], refs[2 * n_stacks :]
    stack_refs, grads_refs = refs[:n_stacks], refs[n_stacks:]
    step = late_ref.shape[0]
    pre = pre_of(stack_refs[0], weights[0], weights[1], x_ref)
    grads = grads_of(pre, prev_ref[...])
    terms_of(early_ref, late_ref, hidden_of(pre), grads, x_ref, g_ref)
    both = jnp.concatenate([own_ref[...], grads], axis=0)
    if halves == 1:
        grads_refs[0][...] = both
        return
    half = both.shape[1] // 2

    low, high = both[:, :half], both[:, half:]
    step2 = grads.shape[0]

    @pl.when(index_ref[0] == 0)
    def _():
        grads_refs[0][...] = low
        grads_refs[1][...] = jnp.concatenate([high[step2:], high[:step2]], axis=1)

    @pl.when(index_ref[0] != 0)
    def _():
        grads_refs[0][...] = high
        grads_refs[1][...] = jnp.concatenate([low[step2:], low[:step2]], axis=1)

    for n in range(1, n_stacks):
        for at in columns(x_ref.shape[1]):
            gate, up = weights[2 * n][:, at], weights[2 * n + 1][:, at]
            stack_refs[n][:, at] = stacked(gate, up, step)


def second_meeting(x, g, grad_hidden, own_grads, weights, index, halves):
    rows, width = x.shape
    step2 = own_grads.shape[0]
    n_stacks = len(weights) // 2
    return pl.pallas_call(
        functools.partial(second_kernel, n_stacks, halves),
        in_specs=[VMEM] * 4 + [SMEM] + [VMEM] * len(weights),
        out_specs=[VMEM] * (2 + n_stacks + halves),
        out_shape=[pltpu.VMEM((step2, width), BF16), pltpu.VMEM((step2 // 2, width), BF16)]
        + [pltpu.VMEM((step2, width), BF16)] * n_stacks
        + [pltpu.VMEM((2 * step2, rows // halves), BF16), pltpu.VMEM((step2, rows), BF16)][:halves],
        name="second_meeting",
        **params(6 * step2 * rows * width, 4 * rows * width),
    )(*in_vmem(x, g, grad_hidden, own_grads), index.reshape(1), *in_vmem(*weights))


def stack_kernel(gate_ref, up_ref, after_ref, out_ref):
    del after_ref
    for at in columns(out_ref.shape[1]):
        out_ref[:, at] = stacked(gate_ref[:, at], up_ref[:, at], out_ref.shape[0] // 2)


def stack(w_gate, w_up, step, after):
    width = w_gate.shape[1]
    return pl.pallas_call(
        stack_kernel,
        in_specs=[VMEM, VMEM, ANY],
        out_specs=VMEM,
        out_shape=pltpu.VMEM((2 * step, width), BF16),
        name="stack",
        **params(0, 8 * step * width),
    )(*in_vmem(w_gate, w_up), after)


def sums_kernel(x_ref, g_ref, hidden_ref, grads_ref, after_ref, early_ref, late_ref):
    del after_ref
    terms_of(early_ref, late_ref, hidden_ref[...], grads_ref[...], x_ref, g_ref)


def own_sums(x, g, hidden, grads, after):
    rows, width = x.shape
    return pl.pallas_call(
        sums_kernel,
        in_specs=[VMEM] * 4 + [ANY],
        out_specs=[VMEM] * 2,
        out_shape=[pltpu.VMEM((n * hidden.shape[0], width), F32) for n in (2, 1)],
        name="own_sums",
        **params(6 * hidden.shape[0] * rows * width, 4 * rows * width),
    )(*in_vmem(x, g, hidden, grads), after)


def total_kernel(own_ref, back_ref, after_ref, *refs):
    del after_ref
    out_refs, (total_ref, sem) = refs[:-2], refs[-2:]
    step, hidden = own_ref.shape[0] // len(out_refs), out_refs[0].shape[0]
    stores = []
    for k, out_ref in enumerate(out_refs):
        for first in range(0, step, 8):
            part = pl.ds(k * step + first, 8)
            total_ref[part, :] = own_ref[part, :] + back_ref[part, :].astype(F32)
            for r in range(first, min(first + 8, hidden)):
                row = total_ref.at[pl.ds(k * step + r, 1), :]
                stores.append(pltpu.make_async_copy(row, out_ref.at[r], sem.at[k, r]))
                stores[-1].start()
    for copy in stores:
        copy.wait()


def totals(own, back, count, hidden, after, place=HBM):
    rows, width = own.shape
    return pl.pallas_call(
        total_kernel,
        in_specs=[VMEM, VMEM, place],
        out_specs=[HBM] * count,
        out_shape=[jax.ShapeDtypeStruct((hidden, 1, width), F32)] * count,
        scratch_shapes=[
            pltpu.VMEM((rows, width), F32),
            pltpu.SemaphoreType.DMA((count, hidden)),
        ],
        name="totals",
        **params(rows * width, 10 * rows * width),
    )(*in_vmem(own, back), pltpu.with_memory_space_constraint(after, pltpu.HBM) if place is HBM else after)


def in_grad_kernel(left_counts, right_counts, after_ref, *refs):
    del after_ref
    *refs, out_ref, scratch, sem = refs
    stores = []
    for n, at in enumerate(columns(out_ref.shape[1])):
        rest = list(refs)
        result = None
        for n_left, groups in zip(left_counts, right_counts):
            left = [rest.pop(0)[...] for _ in range(n_left)]
            right = []
            for count in groups:
                term = rest.pop(0)[:, at]
                for _ in range(count - 1):
                    term = term + rest.pop(0)[:, at]
                right.append(term)
            partial = lax.dot_general(
                jnp.concatenate(left, axis=0),
                jnp.concatenate(right, axis=0),
                (((0,), (0,)), ((), ())),
                preferred_element_type=F32,
            )
            partial = partial.astype(BF16).astype(F32)
            result = partial if result is None else result + partial
        scratch[:, at] = result.astype(BF16)
        stores.append(pltpu.make_async_copy(scratch.at[:, at], out_ref.at[:, at], sem.at[n]))
        stores[-1].start()
    for copy in stores:
        copy.wait()


def in_grad_of(after, *partials):
    operands = []
    for lefts, rights in partials:
        operands += lefts + [t for r in rights for t in r]
    rows, width = partials[0][0][0].shape[1], partials[0][1][0][0].shape[1]
    return pl.pallas_call(
        functools.partial(
            in_grad_kernel,
            [len(l) for l, _ in partials],
            [[len(t) for t in r] for _, r in partials],
        ),
        in_specs=[HBM] + [VMEM] * len(operands),
        out_specs=HBM,
        out_shape=jax.ShapeDtypeStruct((rows, width), BF16),
        scratch_shapes=[
            pltpu.VMEM((rows, width), BF16),
            pltpu.SemaphoreType.DMA((len(columns(width)),)),
        ],
        name="in_grad",
        **params(
            2 * sum(t.shape[0] for l, _ in partials for t in l) * rows * width,
            2 * sum(t.size for t in operands) + 2 * rows * width,
        ),
    )(pltpu.with_memory_space_constraint(after, pltpu.HBM), *in_vmem(*operands))


def dot_left(left, right):
    return lax.dot_general(left, right, (((0,), (0,)), ((), ())), preferred_element_type=F32)


def ready_part_kernel(mine_ref, own_ref, prev_ref, theirs_ref, other_ref, after_ref, mine_out, theirs_out, done_ref):
    del after_ref
    done_ref[...] = jnp.zeros_like(done_ref)
    for at in columns(own_ref.shape[1]):
        both = jnp.concatenate([own_ref[:, at], prev_ref[:, at]], axis=0)
        mine_out[:, at] = dot_left(mine_ref[...], both).astype(BF16)
        theirs_out[:, at] = dot_left(theirs_ref[:, theirs_out.shape[0] :], other_ref[:, at])


def ready_part(mine, own, prev, theirs, other, after):
    rows, width = mine.shape[1], own.shape[1]
    return pl.pallas_call(
        ready_part_kernel,
        in_specs=[VMEM] * 5 + [ANY],
        out_specs=[VMEM] * 3,
        out_shape=[
            pltpu.VMEM((rows, width), BF16),
            pltpu.VMEM((rows, width), F32),
            pltpu.VMEM((8, 128), F32),
        ],
        name="ready_part",
        **params(6 * other.shape[0] * rows * width, 6 * rows * width),
    )(*in_vmem(mine, own, prev, theirs, other), after)


def add_rows(total_ref, own_ref, back_ref, first_row, out_ref, sem):
    hidden, stores = out_ref.shape[0], []
    for first in range(0, hidden, 8):
        part = pl.ds(first_row + first, 8)
        total_ref[part, :] = own_ref[part, :] + back_ref[part, :].astype(F32)
        for r in range(first, min(first + 8, hidden)):
            row = total_ref.at[pl.ds(first_row + r, 1), :]
            stores.append(pltpu.make_async_copy(row, out_ref.at[r], sem.at[r]))
            stores[-1].start()
    return stores


def last_kernel(mine_ref, part_ref, theirs_ref, even_ref, odd_ref, own_ref, back_ref, after_ref, out_ref, up_ref, scratch, total_ref, sem, up_sem):
    del after_ref
    stores = add_rows(total_ref, own_ref, back_ref, 0, up_ref, up_sem)
    for n, at in enumerate(columns(out_ref.shape[1])):
        term = dot_left(theirs_ref[:, : out_ref.shape[0]], even_ref[:, at] + odd_ref[:, at])
        theirs = (part_ref[:, at] + term).astype(BF16)
        scratch[:, at] = (mine_ref[:, at].astype(F32) + theirs.astype(F32)).astype(BF16)
        stores.append(pltpu.make_async_copy(scratch.at[:, at], out_ref.at[:, at], sem.at[n]))
        stores[-1].start()
    for copy in stores:
        copy.wait()


def last_part(mine_partial, part, theirs, even, odd, own, back, hidden, after):
    rows, width = part.shape
    return pl.pallas_call(
        last_kernel,
        in_specs=[VMEM] * 7 + [HBM],
        out_specs=[HBM] * 2,
        out_shape=[
            jax.ShapeDtypeStruct((rows, width), BF16),
            jax.ShapeDtypeStruct((hidden, 1, width), F32),
        ],
        scratch_shapes=[
            pltpu.VMEM((rows, width), BF16),
            pltpu.VMEM(own.shape, F32),
            pltpu.SemaphoreType.DMA((len(columns(width)),)),
            pltpu.SemaphoreType.DMA((hidden,)),
        ],
        name="last_part",
        **params(2 * even.shape[0] * rows * width, 8 * rows * width),
    )(
        *in_vmem(mine_partial, part, theirs, even, odd, own, back),
        pltpu.with_memory_space_constraint(after, pltpu.HBM),
    )


def local(activations, out_grad, gate_weight, up_weight, down_weight):
    n_blk, n_tensor = lax.axis_size("blk"), lax.axis_size("tensor")
    hidden = gate_weight.shape[2]
    step = -(-hidden // 8) * 8
    pairs = n_tensor == 2 and n_blk % 2 == 0
    w_gate, w_up, w_down = gate_weight[0].T, up_weight[0].T, down_weight[0]
    prev_down, prev_gate, prev_up = [from_behind(w, "blk", 1) for w in (w_down, w_gate, w_up)]
    weights = [prev_gate, prev_up]
    if pairs:
        axes = ("blk", "tensor")
        swap = [(0, 1), (1, 0)]
        on_chip = [(2 * b + j, 2 * (b + 1) + j) for b in range(0, n_blk, 2) for j in range(2)]
        across = [(2 * b + j, 2 * b + 1 - j) for b in range(0, n_blk, 2) for j in range(2)]
        other_gate, other_up = [lax.ppermute(w, "tensor", swap) for w in (w_gate, w_up)]

    w_gu, own_grads, own_hidden = own_meeting(activations, out_grad, w_gate, w_up, w_down, step)
    grad_hidden = grad_hidden_of(out_grad, prev_down, own_grads)
    early, late, prev_gu, *grads = second_meeting(
        activations,
        out_grad,
        grad_hidden,
        own_grads,
        weights,
        lax.axis_index("tensor"),
        2 if pairs else 1,
    )
    back_early, back_late = [from_behind(t, "blk", -1) for t in (early, late)]
    sums_early, sums_late = own_sums(activations, out_grad, own_hidden, own_grads, back_early)
    if pairs:
        mine, sent = grads
        prev_other_even = lax.ppermute(prev_gu, axes, across)
        theirs = lax.ppermute(sent, "tensor", swap)
        other_gu = stack(other_gate, other_up, step, theirs)
        prev_other_odd = lax.ppermute(other_gu, axes, on_chip)
        mine_partial, part, done = ready_part(mine, w_gu, prev_gu, theirs, other_gu, sums_late)
    else:
        done = prev_gu
    total_down, total_gate = totals(sums_early, back_early, 2, hidden, activations)
    if pairs:
        in_grad, total_up = last_part(
            mine_partial,
            part,
            theirs,
            prev_other_even,
            prev_other_odd,
            sums_late,
            back_late,
            hidden,
            total_gate,
        )
    else:
        after = in_grad_of(activations, (grads, [[w_gu], [prev_gu]]))
        in_grad = lax.psum_scatter(after, "tensor", scatter_dimension=0, tiled=True)
        [total_up] = totals(sums_late, back_late, 1, hidden, after)
    return (
        in_grad,
        total_gate.transpose(1, 2, 0),
        total_up.transpose(1, 2, 0),
        total_down.transpose(1, 0, 2),
    )


def solution(mesh):
    in_specs = (
        P("blk", None),
        P("blk", None),
        P("blk", None, "tensor"),
        P("blk", None, "tensor"),
        P("blk", "tensor", None),
    )
    out_specs = (
        P(("blk", "tensor"), None),
        P("blk", None, "tensor"),
        P("blk", None, "tensor"),
        P("blk", "tensor", None),
    )
    return jax.shard_map(local, mesh=mesh, in_specs=in_specs, out_specs=out_specs, check_vma=False)
```

```python
import functools

import jax
import jax.numpy as jnp
from jax import lax
from jax.experimental import pallas as pl
from jax.experimental.pallas import tpu as pltpu
from jax.sharding import PartitionSpec as P

F32 = jnp.float32
BF16 = jnp.bfloat16
VMEM_LIMIT = 16 * 2**20
VMEM = pl.BlockSpec(memory_space=pltpu.VMEM)
ANY = pl.BlockSpec(memory_space=pl.ANY)
HBM = pl.BlockSpec(memory_space=pltpu.HBM)
SMEM = pl.BlockSpec(memory_space=pltpu.SMEM)


def from_behind(value, axis, by):
    devices = lax.axis_size(axis)
    return lax.ppermute(value, axis, [(i, (i + by) % devices) for i in range(devices)])


def column_block(width, limit):
    block = limit
    while width % block:
        block -= 128
    return block


def columns(width, limit=1024):
    block = column_block(width, limit)
    return [pl.ds(at, block) for at in range(0, width, block)]


def in_vmem(*arrays):
    return [pltpu.with_memory_space_constraint(a, pltpu.VMEM) for a in arrays]


def params(flops, nbytes):
    return dict(
        compiler_params=pltpu.CompilerParams(vmem_limit_bytes=VMEM_LIMIT),
        cost_estimate=pl.CostEstimate(flops=flops, bytes_accessed=nbytes, transcendentals=0),
    )


def stacked(gate, up, step):
    if gate.shape[0] == step:
        return jnp.concatenate([gate, up], axis=0)
    pad = jnp.zeros((step - gate.shape[0], gate.shape[1]), gate.dtype)
    return jnp.concatenate([gate, pad, up, pad], axis=0)


def pre_of(stack_ref, gate_ref, up_ref, rows_ref):
    total = None
    for at in columns(stack_ref.shape[1]):
        weight = stacked(gate_ref[:, at], up_ref[:, at], stack_ref.shape[0] // 2)
        stack_ref[:, at] = weight
        term = lax.dot_general(
            weight, rows_ref[:, at], (((1,), (1,)), ((), ())), preferred_element_type=F32
        )
        total = term if total is None else total + term
    return total


def hidden_of(pre):
    step = pre.shape[0] // 2
    gate_pre, up_pre = pre[:step], pre[step:]
    return (gate_pre * jax.nn.sigmoid(gate_pre) * up_pre).astype(BF16)


def product(weight_ref, rows_ref):
    total = None
    for at in columns(weight_ref.shape[1]):
        term = lax.dot_general(
            weight_ref[:, at], rows_ref[:, at], (((1,), (1,)), ((), ())), preferred_element_type=F32
        )
        total = term if total is None else total + term
    return total


def grads_of(pre, grad_hidden):
    step, hidden = pre.shape[0] // 2, grad_hidden.shape[0]
    if step > hidden:
        pad = jnp.zeros((step - hidden, grad_hidden.shape[1]), F32)
        grad_hidden = jnp.concatenate([grad_hidden, pad], axis=0)
    gate_pre, up_pre = pre[:step], pre[step:]
    sigmoid_part = jax.nn.sigmoid(gate_pre)
    slope_part = sigmoid_part * (1.0 + gate_pre * (1.0 - sigmoid_part))
    grad_gate = (grad_hidden * up_pre * slope_part).astype(BF16)
    grad_up = (grad_hidden * (gate_pre * sigmoid_part)).astype(BF16)
    return jnp.concatenate([grad_gate, grad_up], axis=0)


def terms_of(early_ref, late_ref, hidden, grads, x_ref, g_ref):
    step = hidden.shape[0]
    for at in columns(x_ref.shape[1]):
        down = jnp.dot(hidden, g_ref[:, at], preferred_element_type=F32)
        gate_up = jnp.dot(grads, x_ref[:, at], preferred_element_type=F32)
        early = jnp.concatenate([down, gate_up[:step]], axis=0)
        early_ref[:, at] = early.astype(early_ref.dtype)
        late_ref[:, at] = gate_up[step:].astype(late_ref.dtype)


def own_kernel(x_ref, g_ref, gate_in, up_in, down_in, stack_ref, grads_ref, hidden_ref, gate_ref, up_ref, down_ref, sem):
    copies = [
        pltpu.make_async_copy(source, into, sem.at[n])
        for n, (source, into) in enumerate(
            [(gate_in, gate_ref), (up_in, up_ref), (down_in, down_ref)]
        )
    ]
    for copy in copies:
        copy.start()
    copies[0].wait()
    copies[1].wait()
    pre = pre_of(stack_ref, gate_ref, up_ref, x_ref)
    hidden_ref[...] = hidden_of(pre)
    copies[2].wait()
    grads_ref[...] = grads_of(pre, product(down_ref, g_ref))


def own_meeting(x, g, w_gate, w_up, w_down, step):
    rows, width = x.shape
    weights = [pltpu.with_memory_space_constraint(w, pltpu.HBM) for w in (w_gate, w_up, w_down)]
    return pl.pallas_call(
        own_kernel,
        in_specs=[VMEM] * 2 + [HBM] * 3,
        out_specs=[VMEM] * 3,
        out_shape=[
            pltpu.VMEM((2 * step, width), BF16),
            pltpu.VMEM((2 * step, rows), BF16),
            pltpu.VMEM((step, rows), BF16),
        ],
        scratch_shapes=[pltpu.VMEM(w_gate.shape, BF16)] * 3 + [pltpu.SemaphoreType.DMA((3,))],
        name="own_meeting",
        **params(6 * step * rows * width, 4 * rows * width),
    )(*in_vmem(x, g), *weights)


def grad_hidden_kernel(g_ref, down_ref, after_ref, out_ref):
    del after_ref
    out_ref[...] = product(down_ref, g_ref)


def grad_hidden_of(g, w_down, after):
    rows, width = g.shape
    return pl.pallas_call(
        grad_hidden_kernel,
        in_specs=[VMEM] * 2 + [ANY],
        out_specs=VMEM,
        out_shape=pltpu.VMEM((w_down.shape[0], rows), F32),
        name="grad_hidden",
        **params(2 * w_down.size * rows, 2 * g.size),
    )(*in_vmem(g, w_down), after)


def second_kernel(n_stacks, halves, x_ref, g_ref, prev_ref, own_ref, index_ref, *refs):
    weights, (early_ref, late_ref, *refs) = refs[: 2 * n_stacks], refs[2 * n_stacks :]
    stack_refs, grads_refs = refs[:n_stacks], refs[n_stacks:]
    step = late_ref.shape[0]
    pre = pre_of(stack_refs[0], weights[0], weights[1], x_ref)
    grads = grads_of(pre, prev_ref[...])
    terms_of(early_ref, late_ref, hidden_of(pre), grads, x_ref, g_ref)
    both = jnp.concatenate([own_ref[...], grads], axis=0)
    if halves == 1:
        grads_refs[0][...] = both
        return
    half = both.shape[1] // 2

    @pl.when(index_ref[0] == 0)
    def _():
        grads_refs[0][...] = both[:, :half]
        grads_refs[1][...] = both[:, half:]

    @pl.when(index_ref[0] != 0)
    def _():
        grads_refs[0][...] = both[:, half:]
        grads_refs[1][...] = both[:, :half]

    for n in range(1, n_stacks):
        for at in columns(x_ref.shape[1]):
            gate, up = weights[2 * n][:, at], weights[2 * n + 1][:, at]
            stack_refs[n][:, at] = stacked(gate, up, step)


def second_meeting(x, g, grad_hidden, own_grads, weights, index, halves):
    rows, width = x.shape
    step2 = own_grads.shape[0]
    n_stacks = len(weights) // 2
    return pl.pallas_call(
        functools.partial(second_kernel, n_stacks, halves),
        in_specs=[VMEM] * 4 + [SMEM] + [VMEM] * len(weights),
        out_specs=[VMEM] * (2 + n_stacks + halves),
        out_shape=[pltpu.VMEM((step2, width), BF16), pltpu.VMEM((step2 // 2, width), BF16)]
        + [pltpu.VMEM((step2, width), BF16)] * n_stacks
        + [pltpu.VMEM((2 * step2, rows // halves), BF16)] * halves,
        name="second_meeting",
        **params(6 * step2 * rows * width, 4 * rows * width),
    )(*in_vmem(x, g, grad_hidden, own_grads), index.reshape(1), *in_vmem(*weights))


def stack_kernel(gate_ref, up_ref, after_ref, out_ref):
    del after_ref
    for at in columns(out_ref.shape[1]):
        out_ref[:, at] = stacked(gate_ref[:, at], up_ref[:, at], out_ref.shape[0] // 2)


def stack(w_gate, w_up, step, after):
    width = w_gate.shape[1]
    return pl.pallas_call(
        stack_kernel,
        in_specs=[VMEM, VMEM, ANY],
        out_specs=VMEM,
        out_shape=pltpu.VMEM((2 * step, width), BF16),
        name="stack",
        **params(0, 8 * step * width),
    )(*in_vmem(w_gate, w_up), after)


def sums_kernel(x_ref, g_ref, hidden_ref, grads_ref, after_ref, early_ref, late_ref):
    del after_ref
    terms_of(early_ref, late_ref, hidden_ref[...], grads_ref[...], x_ref, g_ref)


def own_sums(x, g, hidden, grads, after):
    rows, width = x.shape
    return pl.pallas_call(
        sums_kernel,
        in_specs=[VMEM] * 4 + [ANY],
        out_specs=[VMEM] * 2,
        out_shape=[pltpu.VMEM((n * hidden.shape[0], width), F32) for n in (2, 1)],
        name="own_sums",
        **params(6 * hidden.shape[0] * rows * width, 4 * rows * width),
    )(*in_vmem(x, g, hidden, grads), after)


def total_kernel(own_ref, back_ref, after_ref, *refs):
    del after_ref
    out_refs, (total_ref, sem) = refs[:-2], refs[-2:]
    step, hidden = own_ref.shape[0] // len(out_refs), out_refs[0].shape[0]
    stores = []
    for k, out_ref in enumerate(out_refs):
        for first in range(0, step, 8):
            part = pl.ds(k * step + first, 8)
            total_ref[part, :] = own_ref[part, :] + back_ref[part, :].astype(F32)
            for r in range(first, min(first + 8, hidden)):
                row = total_ref.at[pl.ds(k * step + r, 1), :]
                stores.append(pltpu.make_async_copy(row, out_ref.at[r], sem.at[k, r]))
                stores[-1].start()
    for copy in stores:
        copy.wait()


def totals(own, back, count, hidden, after, place=HBM):
    rows, width = own.shape
    return pl.pallas_call(
        total_kernel,
        in_specs=[VMEM, VMEM, place],
        out_specs=[HBM] * count,
        out_shape=[jax.ShapeDtypeStruct((hidden, 1, width), F32)] * count,
        scratch_shapes=[
            pltpu.VMEM((rows, width), F32),
            pltpu.SemaphoreType.DMA((count, hidden)),
        ],
        name="totals",
        **params(rows * width, 10 * rows * width),
    )(*in_vmem(own, back), pltpu.with_memory_space_constraint(after, pltpu.HBM) if place is HBM else after)


def in_grad_kernel(left_counts, right_counts, after_ref, *refs):
    del after_ref
    *refs, out_ref, scratch, sem = refs
    stores = []
    for n, at in enumerate(columns(out_ref.shape[1])):
        rest = list(refs)
        result = None
        for n_left, groups in zip(left_counts, right_counts):
            left = [rest.pop(0)[...] for _ in range(n_left)]
            right = []
            for count in groups:
                term = rest.pop(0)[:, at]
                for _ in range(count - 1):
                    term = term + rest.pop(0)[:, at]
                right.append(term)
            partial = lax.dot_general(
                jnp.concatenate(left, axis=0),
                jnp.concatenate(right, axis=0),
                (((0,), (0,)), ((), ())),
                preferred_element_type=F32,
            )
            partial = partial.astype(BF16).astype(F32)
            result = partial if result is None else result + partial
        scratch[:, at] = result.astype(BF16)
        stores.append(pltpu.make_async_copy(scratch.at[:, at], out_ref.at[:, at], sem.at[n]))
        stores[-1].start()
    for copy in stores:
        copy.wait()


def in_grad_of(after, *partials):
    operands = []
    for lefts, rights in partials:
        operands += lefts + [t for r in rights for t in r]
    rows, width = partials[0][0][0].shape[1], partials[0][1][0][0].shape[1]
    return pl.pallas_call(
        functools.partial(
            in_grad_kernel,
            [len(l) for l, _ in partials],
            [[len(t) for t in r] for _, r in partials],
        ),
        in_specs=[HBM] + [VMEM] * len(operands),
        out_specs=HBM,
        out_shape=jax.ShapeDtypeStruct((rows, width), BF16),
        scratch_shapes=[
            pltpu.VMEM((rows, width), BF16),
            pltpu.SemaphoreType.DMA((len(columns(width)),)),
        ],
        name="in_grad",
        **params(
            2 * sum(t.shape[0] for l, _ in partials for t in l) * rows * width,
            2 * sum(t.size for t in operands) + 2 * rows * width,
        ),
    )(pltpu.with_memory_space_constraint(after, pltpu.HBM), *in_vmem(*operands))


def dot_left(left, right):
    return lax.dot_general(left, right, (((0,), (0,)), ((), ())), preferred_element_type=F32)


def ready_part_kernel(mine_ref, own_ref, prev_ref, theirs_ref, other_ref, after_ref, mine_out, theirs_out, done_ref):
    del after_ref
    step2 = other_ref.shape[0]
    done_ref[...] = jnp.zeros_like(done_ref)
    for at in columns(own_ref.shape[1]):
        both = jnp.concatenate([own_ref[:, at], prev_ref[:, at]], axis=0)
        mine_out[:, at] = dot_left(mine_ref[...], both).astype(BF16)
        theirs_out[:, at] = dot_left(theirs_ref[:step2, :], other_ref[:, at])


def ready_part(mine, own, prev, theirs, other, after):
    rows, width = mine.shape[1], own.shape[1]
    return pl.pallas_call(
        ready_part_kernel,
        in_specs=[VMEM] * 5 + [ANY],
        out_specs=[VMEM] * 3,
        out_shape=[
            pltpu.VMEM((rows, width), BF16),
            pltpu.VMEM((rows, width), F32),
            pltpu.VMEM((8, 128), F32),
        ],
        name="ready_part",
        **params(6 * other.shape[0] * rows * width, 6 * rows * width),
    )(*in_vmem(mine, own, prev, theirs, other), after)


def add_rows(total_ref, own_ref, back_ref, first_row, out_ref, sem):
    hidden, stores = out_ref.shape[0], []
    for first in range(0, hidden, 8):
        part = pl.ds(first_row + first, 8)
        total_ref[part, :] = own_ref[part, :] + back_ref[part, :].astype(F32)
        for r in range(first, min(first + 8, hidden)):
            row = total_ref.at[pl.ds(first_row + r, 1), :]
            stores.append(pltpu.make_async_copy(row, out_ref.at[r], sem.at[r]))
            stores[-1].start()
    return stores


def last_kernel(mine_ref, part_ref, theirs_ref, even_ref, odd_ref, own_ref, back_ref, after_ref, out_ref, up_ref, scratch, total_ref, sem, up_sem):
    del after_ref
    stores = add_rows(total_ref, own_ref, back_ref, 0, up_ref, up_sem)
    for n, at in enumerate(columns(out_ref.shape[1])):
        term = dot_left(theirs_ref[even_ref.shape[0] :, :], even_ref[:, at] + odd_ref[:, at])
        theirs = (part_ref[:, at] + term).astype(BF16)
        scratch[:, at] = (mine_ref[:, at].astype(F32) + theirs.astype(F32)).astype(BF16)
        stores.append(pltpu.make_async_copy(scratch.at[:, at], out_ref.at[:, at], sem.at[n]))
        stores[-1].start()
    for copy in stores:
        copy.wait()


def last_part(mine_partial, part, theirs, even, odd, own, back, hidden, after):
    rows, width = part.shape
    return pl.pallas_call(
        last_kernel,
        in_specs=[VMEM] * 7 + [HBM],
        out_specs=[HBM] * 2,
        out_shape=[
            jax.ShapeDtypeStruct((rows, width), BF16),
            jax.ShapeDtypeStruct((hidden, 1, width), F32),
        ],
        scratch_shapes=[
            pltpu.VMEM((rows, width), BF16),
            pltpu.VMEM(own.shape, F32),
            pltpu.SemaphoreType.DMA((len(columns(width)),)),
            pltpu.SemaphoreType.DMA((hidden,)),
        ],
        name="last_part",
        **params(2 * even.shape[0] * rows * width, 8 * rows * width),
    )(
        *in_vmem(mine_partial, part, theirs, even, odd, own, back),
        pltpu.with_memory_space_constraint(after, pltpu.HBM),
    )


def local(activations, out_grad, gate_weight, up_weight, down_weight):
    n_blk, n_tensor = lax.axis_size("blk"), lax.axis_size("tensor")
    hidden = gate_weight.shape[2]
    step = -(-hidden // 8) * 8
    pairs = n_tensor == 2 and n_blk % 2 == 0
    w_gate, w_up, w_down = gate_weight[0].T, up_weight[0].T, down_weight[0]
    prev_down, prev_gate, prev_up = [from_behind(w, "blk", 1) for w in (w_down, w_gate, w_up)]
    weights = [prev_gate, prev_up]
    if pairs:
        axes = ("blk", "tensor")
        swap = [(0, 1), (1, 0)]
        on_chip = [(2 * b + j, 2 * (b + 1) + j) for b in range(0, n_blk, 2) for j in range(2)]
        across = [(2 * b + j, 2 * b + 1 - j) for b in range(0, n_blk, 2) for j in range(2)]
        other_gate, other_up = [lax.ppermute(w, "tensor", swap) for w in (w_gate, w_up)]

    w_gu, own_grads, own_hidden = own_meeting(activations, out_grad, w_gate, w_up, w_down, step)
    grad_hidden = grad_hidden_of(out_grad, prev_down, own_grads)
    early, late, prev_gu, *grads = second_meeting(
        activations,
        out_grad,
        grad_hidden,
        own_grads,
        weights,
        lax.axis_index("tensor"),
        2 if pairs else 1,
    )
    back_early, back_late = [from_behind(t, "blk", -1) for t in (early, late)]
    sums_early, sums_late = own_sums(activations, out_grad, own_hidden, own_grads, back_early)
    if pairs:
        mine, sent = grads
        prev_other_even = lax.ppermute(prev_gu, axes, across)
        theirs = lax.ppermute(sent, "tensor", swap)
        other_gu = stack(other_gate, other_up, step, theirs)
        prev_other_odd = lax.ppermute(other_gu, axes, on_chip)
        mine_partial, part, done = ready_part(mine, w_gu, prev_gu, theirs, other_gu, sums_late)
    else:
        done = prev_gu
    total_down, total_gate = totals(sums_early, back_early, 2, hidden, activations)
    if pairs:
        in_grad, total_up = last_part(
            mine_partial,
            part,
            theirs,
            prev_other_even,
            prev_other_odd,
            sums_late,
            back_late,
            hidden,
            total_gate,
        )
    else:
        after = in_grad_of(activations, (grads, [[w_gu], [prev_gu]]))
        in_grad = lax.psum_scatter(after, "tensor", scatter_dimension=0, tiled=True)
        [total_up] = totals(sums_late, back_late, 1, hidden, after)
    return (
        in_grad,
        total_gate.transpose(1, 2, 0),
        total_up.transpose(1, 2, 0),
        total_down.transpose(1, 0, 2),
    )


def solution(mesh):
    in_specs = (
        P("blk", None),
        P("blk", None),
        P("blk", None, "tensor"),
        P("blk", None, "tensor"),
        P("blk", "tensor", None),
    )
    out_specs = (
        P(("blk", "tensor"), None),
        P("blk", None, "tensor"),
        P("blk", None, "tensor"),
        P("blk", "tensor", None),
    )
    return jax.shard_map(local, mesh=mesh, in_specs=in_specs, out_specs=out_specs, check_vma=False)
```

```python
import functools

import jax
import jax.numpy as jnp
from jax import lax
from jax.experimental import pallas as pl
from jax.experimental.pallas import tpu as pltpu
from jax.sharding import PartitionSpec as P

F32 = jnp.float32
BF16 = jnp.bfloat16
VMEM_LIMIT = 16 * 2**20
VMEM = pl.BlockSpec(memory_space=pltpu.VMEM)
ANY = pl.BlockSpec(memory_space=pl.ANY)
HBM = pl.BlockSpec(memory_space=pltpu.HBM)
SMEM = pl.BlockSpec(memory_space=pltpu.SMEM)


def from_behind(value, axis, by):
    devices = lax.axis_size(axis)
    return lax.ppermute(value, axis, [(i, (i + by) % devices) for i in range(devices)])


def column_block(width, limit):
    block = limit
    while width % block:
        block -= 128
    return block


def columns(width, limit=1280):
    block = column_block(width, limit)
    return [pl.ds(at, block) for at in range(0, width, block)]


def in_vmem(*arrays):
    return [pltpu.with_memory_space_constraint(a, pltpu.VMEM) for a in arrays]


def params(flops, nbytes):
    return dict(
        compiler_params=pltpu.CompilerParams(vmem_limit_bytes=VMEM_LIMIT),
        cost_estimate=pl.CostEstimate(flops=flops, bytes_accessed=nbytes, transcendentals=0),
    )


def stacked(gate, up, step):
    if gate.shape[0] == step:
        return jnp.concatenate([gate, up], axis=0)
    pad = jnp.zeros((step - gate.shape[0], gate.shape[1]), gate.dtype)
    return jnp.concatenate([gate, pad, up, pad], axis=0)


def pre_of(stack_ref, gate_ref, up_ref, rows_ref):
    total = None
    for at in columns(stack_ref.shape[1]):
        weight = stacked(gate_ref[:, at], up_ref[:, at], stack_ref.shape[0] // 2)
        stack_ref[:, at] = weight
        term = lax.dot_general(
            weight, rows_ref[:, at], (((1,), (1,)), ((), ())), preferred_element_type=F32
        )
        total = term if total is None else total + term
    return total


def hidden_of(pre):
    step = pre.shape[0] // 2
    gate_pre, up_pre = pre[:step], pre[step:]
    return (gate_pre * jax.nn.sigmoid(gate_pre) * up_pre).astype(BF16)


def product(weight_ref, rows_ref):
    total = None
    for at in columns(weight_ref.shape[1]):
        term = lax.dot_general(
            weight_ref[:, at], rows_ref[:, at], (((1,), (1,)), ((), ())), preferred_element_type=F32
        )
        total = term if total is None else total + term
    return total


def grads_of(pre, grad_hidden):
    step, hidden = pre.shape[0] // 2, grad_hidden.shape[0]
    if step > hidden:
        pad = jnp.zeros((step - hidden, grad_hidden.shape[1]), F32)
        grad_hidden = jnp.concatenate([grad_hidden, pad], axis=0)
    gate_pre, up_pre = pre[:step], pre[step:]
    sigmoid_part = jax.nn.sigmoid(gate_pre)
    slope_part = sigmoid_part * (1.0 + gate_pre * (1.0 - sigmoid_part))
    grad_gate = (grad_hidden * up_pre * slope_part).astype(BF16)
    grad_up = (grad_hidden * (gate_pre * sigmoid_part)).astype(BF16)
    return jnp.concatenate([grad_gate, grad_up], axis=0)


def terms_of(early_ref, late_ref, hidden, grads, x_ref, g_ref):
    step = hidden.shape[0]
    for at in columns(x_ref.shape[1]):
        down = jnp.dot(hidden, g_ref[:, at], preferred_element_type=F32)
        gate_up = jnp.dot(grads, x_ref[:, at], preferred_element_type=F32)
        early = jnp.concatenate([down, gate_up[:step]], axis=0)
        early_ref[:, at] = early.astype(early_ref.dtype)
        late_ref[:, at] = gate_up[step:].astype(late_ref.dtype)


def own_kernel(x_ref, g_ref, gate_in, up_in, down_in, stack_ref, grads_ref, hidden_ref, gate_ref, up_ref, down_ref, sem):
    copies = [
        pltpu.make_async_copy(source, into, sem.at[n])
        for n, (source, into) in enumerate(
            [(gate_in, gate_ref), (up_in, up_ref), (down_in, down_ref)]
        )
    ]
    for copy in copies:
        copy.start()
    copies[0].wait()
    copies[1].wait()
    pre = pre_of(stack_ref, gate_ref, up_ref, x_ref)
    hidden_ref[...] = hidden_of(pre)
    copies[2].wait()
    grads_ref[...] = grads_of(pre, product(down_ref, g_ref))


def own_meeting(x, g, w_gate, w_up, w_down, step):
    rows, width = x.shape
    weights = [pltpu.with_memory_space_constraint(w, pltpu.HBM) for w in (w_gate, w_up, w_down)]
    return pl.pallas_call(
        own_kernel,
        in_specs=[VMEM] * 2 + [HBM] * 3,
        out_specs=[VMEM] * 3,
        out_shape=[
            pltpu.VMEM((2 * step, width), BF16),
            pltpu.VMEM((2 * step, rows), BF16),
            pltpu.VMEM((step, rows), BF16),
        ],
        scratch_shapes=[pltpu.VMEM(w_gate.shape, BF16)] * 3 + [pltpu.SemaphoreType.DMA((3,))],
        name="own_meeting",
        **params(6 * step * rows * width, 4 * rows * width),
    )(*in_vmem(x, g), *weights)


def grad_hidden_kernel(g_ref, down_ref, after_ref, out_ref):
    del after_ref
    out_ref[...] = product(down_ref, g_ref)


def grad_hidden_of(g, w_down, after):
    rows, width = g.shape
    return pl.pallas_call(
        grad_hidden_kernel,
        in_specs=[VMEM] * 2 + [ANY],
        out_specs=VMEM,
        out_shape=pltpu.VMEM((w_down.shape[0], rows), F32),
        name="grad_hidden",
        **params(2 * w_down.size * rows, 2 * g.size),
    )(*in_vmem(g, w_down), after)


def second_kernel(n_stacks, halves, x_ref, g_ref, prev_ref, own_ref, index_ref, *refs):
    weights, (early_ref, late_ref, *refs) = refs[: 2 * n_stacks], refs[2 * n_stacks :]
    stack_refs, grads_refs = refs[:n_stacks], refs[n_stacks:]
    step = late_ref.shape[0]
    pre = pre_of(stack_refs[0], weights[0], weights[1], x_ref)
    grads = grads_of(pre, prev_ref[...])
    terms_of(early_ref, late_ref, hidden_of(pre), grads, x_ref, g_ref)
    both = jnp.concatenate([own_ref[...], grads], axis=0)
    if halves == 1:
        grads_refs[0][...] = both
        return
    half = both.shape[1] // 2

    @pl.when(index_ref[0] == 0)
    def _():
        grads_refs[0][...] = both[:, :half]
        grads_refs[1][...] = both[:, half:]

    @pl.when(index_ref[0] != 0)
    def _():
        grads_refs[0][...] = both[:, half:]
        grads_refs[1][...] = both[:, :half]

    for n in range(1, n_stacks):
        for at in columns(x_ref.shape[1]):
            gate, up = weights[2 * n][:, at], weights[2 * n + 1][:, at]
            stack_refs[n][:, at] = stacked(gate, up, step)


def second_meeting(x, g, grad_hidden, own_grads, weights, index, halves):
    rows, width = x.shape
    step2 = own_grads.shape[0]
    n_stacks = len(weights) // 2
    return pl.pallas_call(
        functools.partial(second_kernel, n_stacks, halves),
        in_specs=[VMEM] * 4 + [SMEM] + [VMEM] * len(weights),
        out_specs=[VMEM] * (2 + n_stacks + halves),
        out_shape=[pltpu.VMEM((step2, width), BF16), pltpu.VMEM((step2 // 2, width), BF16)]
        + [pltpu.VMEM((step2, width), BF16)] * n_stacks
        + [pltpu.VMEM((2 * step2, rows // halves), BF16)] * halves,
        name="second_meeting",
        **params(6 * step2 * rows * width, 4 * rows * width),
    )(*in_vmem(x, g, grad_hidden, own_grads), index.reshape(1), *in_vmem(*weights))


def stack_kernel(gate_ref, up_ref, after_ref, out_ref):
    del after_ref
    for at in columns(out_ref.shape[1]):
        out_ref[:, at] = stacked(gate_ref[:, at], up_ref[:, at], out_ref.shape[0] // 2)


def stack(w_gate, w_up, step, after):
    width = w_gate.shape[1]
    return pl.pallas_call(
        stack_kernel,
        in_specs=[VMEM, VMEM, ANY],
        out_specs=VMEM,
        out_shape=pltpu.VMEM((2 * step, width), BF16),
        name="stack",
        **params(0, 8 * step * width),
    )(*in_vmem(w_gate, w_up), after)


def sums_kernel(x_ref, g_ref, hidden_ref, grads_ref, after_ref, early_ref, late_ref):
    del after_ref
    terms_of(early_ref, late_ref, hidden_ref[...], grads_ref[...], x_ref, g_ref)


def own_sums(x, g, hidden, grads, after):
    rows, width = x.shape
    return pl.pallas_call(
        sums_kernel,
        in_specs=[VMEM] * 4 + [ANY],
        out_specs=[VMEM] * 2,
        out_shape=[pltpu.VMEM((n * hidden.shape[0], width), F32) for n in (2, 1)],
        name="own_sums",
        **params(6 * hidden.shape[0] * rows * width, 4 * rows * width),
    )(*in_vmem(x, g, hidden, grads), after)


def total_kernel(own_ref, back_ref, after_ref, *refs):
    del after_ref
    out_refs, (total_ref, sem) = refs[:-2], refs[-2:]
    step, hidden = own_ref.shape[0] // len(out_refs), out_refs[0].shape[0]
    stores = []
    for k, out_ref in enumerate(out_refs):
        for first in range(0, step, 8):
            part = pl.ds(k * step + first, 8)
            total_ref[part, :] = own_ref[part, :] + back_ref[part, :].astype(F32)
            for r in range(first, min(first + 8, hidden)):
                row = total_ref.at[pl.ds(k * step + r, 1), :]
                stores.append(pltpu.make_async_copy(row, out_ref.at[r], sem.at[k, r]))
                stores[-1].start()
    for copy in stores:
        copy.wait()


def totals(own, back, count, hidden, after, place=HBM):
    rows, width = own.shape
    return pl.pallas_call(
        total_kernel,
        in_specs=[VMEM, VMEM, place],
        out_specs=[HBM] * count,
        out_shape=[jax.ShapeDtypeStruct((hidden, 1, width), F32)] * count,
        scratch_shapes=[
            pltpu.VMEM((rows, width), F32),
            pltpu.SemaphoreType.DMA((count, hidden)),
        ],
        name="totals",
        **params(rows * width, 10 * rows * width),
    )(*in_vmem(own, back), pltpu.with_memory_space_constraint(after, pltpu.HBM) if place is HBM else after)


def in_grad_kernel(left_counts, right_counts, after_ref, *refs):
    del after_ref
    *refs, out_ref, scratch, sem = refs
    stores = []
    for n, at in enumerate(columns(out_ref.shape[1])):
        rest = list(refs)
        result = None
        for n_left, groups in zip(left_counts, right_counts):
            left = [rest.pop(0)[...] for _ in range(n_left)]
            right = []
            for count in groups:
                term = rest.pop(0)[:, at]
                for _ in range(count - 1):
                    term = term + rest.pop(0)[:, at]
                right.append(term)
            partial = lax.dot_general(
                jnp.concatenate(left, axis=0),
                jnp.concatenate(right, axis=0),
                (((0,), (0,)), ((), ())),
                preferred_element_type=F32,
            )
            partial = partial.astype(BF16).astype(F32)
            result = partial if result is None else result + partial
        scratch[:, at] = result.astype(BF16)
        stores.append(pltpu.make_async_copy(scratch.at[:, at], out_ref.at[:, at], sem.at[n]))
        stores[-1].start()
    for copy in stores:
        copy.wait()


def in_grad_of(after, *partials):
    operands = []
    for lefts, rights in partials:
        operands += lefts + [t for r in rights for t in r]
    rows, width = partials[0][0][0].shape[1], partials[0][1][0][0].shape[1]
    return pl.pallas_call(
        functools.partial(
            in_grad_kernel,
            [len(l) for l, _ in partials],
            [[len(t) for t in r] for _, r in partials],
        ),
        in_specs=[HBM] + [VMEM] * len(operands),
        out_specs=HBM,
        out_shape=jax.ShapeDtypeStruct((rows, width), BF16),
        scratch_shapes=[
            pltpu.VMEM((rows, width), BF16),
            pltpu.SemaphoreType.DMA((len(columns(width)),)),
        ],
        name="in_grad",
        **params(
            2 * sum(t.shape[0] for l, _ in partials for t in l) * rows * width,
            2 * sum(t.size for t in operands) + 2 * rows * width,
        ),
    )(pltpu.with_memory_space_constraint(after, pltpu.HBM), *in_vmem(*operands))


def dot_left(left, right):
    return lax.dot_general(left, right, (((0,), (0,)), ((), ())), preferred_element_type=F32)


def ready_part_kernel(mine_ref, own_ref, prev_ref, theirs_ref, other_ref, after_ref, mine_out, theirs_out, done_ref):
    del after_ref
    step2 = other_ref.shape[0]
    done_ref[...] = jnp.zeros_like(done_ref)
    for at in columns(own_ref.shape[1]):
        both = jnp.concatenate([own_ref[:, at], prev_ref[:, at]], axis=0)
        mine_out[:, at] = dot_left(mine_ref[...], both).astype(BF16).astype(F32)
        theirs_out[:, at] = dot_left(theirs_ref[:step2, :], other_ref[:, at])


def ready_part(mine, own, prev, theirs, other, after):
    rows, width = mine.shape[1], own.shape[1]
    return pl.pallas_call(
        ready_part_kernel,
        in_specs=[VMEM] * 5 + [ANY],
        out_specs=[VMEM] * 3,
        out_shape=[
            pltpu.VMEM((rows, width), F32),
            pltpu.VMEM((rows, width), F32),
            pltpu.VMEM((8, 128), F32),
        ],
        name="ready_part",
        **params(6 * other.shape[0] * rows * width, 6 * rows * width),
    )(*in_vmem(mine, own, prev, theirs, other), after)


def add_rows(total_ref, own_ref, back_ref, first_row, out_ref, sem):
    hidden, stores = out_ref.shape[0], []
    for first in range(0, hidden, 8):
        part = pl.ds(first_row + first, 8)
        total_ref[part, :] = own_ref[part, :] + back_ref[part, :].astype(F32)
        for r in range(first, min(first + 8, hidden)):
            row = total_ref.at[pl.ds(first_row + r, 1), :]
            stores.append(pltpu.make_async_copy(row, out_ref.at[r], sem.at[r]))
            stores[-1].start()
    return stores


def last_kernel(mine_ref, part_ref, theirs_ref, even_ref, odd_ref, own_ref, back_ref, after_ref, out_ref, up_ref, scratch, total_ref, sem, up_sem):
    del after_ref
    stores = add_rows(total_ref, own_ref, back_ref, 0, up_ref, up_sem)
    for n, at in enumerate(columns(out_ref.shape[1])):
        term = dot_left(theirs_ref[even_ref.shape[0] :, :], even_ref[:, at] + odd_ref[:, at])
        theirs = (part_ref[:, at] + term).astype(BF16)
        scratch[:, at] = (mine_ref[:, at] + theirs.astype(F32)).astype(BF16)
        stores.append(pltpu.make_async_copy(scratch.at[:, at], out_ref.at[:, at], sem.at[n]))
        stores[-1].start()
    for copy in stores:
        copy.wait()


def last_part(mine_partial, part, theirs, even, odd, own, back, hidden, after):
    rows, width = part.shape
    return pl.pallas_call(
        last_kernel,
        in_specs=[VMEM] * 7 + [HBM],
        out_specs=[HBM] * 2,
        out_shape=[
            jax.ShapeDtypeStruct((rows, width), BF16),
            jax.ShapeDtypeStruct((hidden, 1, width), F32),
        ],
        scratch_shapes=[
            pltpu.VMEM((rows, width), BF16),
            pltpu.VMEM(own.shape, F32),
            pltpu.SemaphoreType.DMA((len(columns(width)),)),
            pltpu.SemaphoreType.DMA((hidden,)),
        ],
        name="last_part",
        **params(2 * even.shape[0] * rows * width, 8 * rows * width),
    )(
        *in_vmem(mine_partial, part, theirs, even, odd, own, back),
        pltpu.with_memory_space_constraint(after, pltpu.HBM),
    )


def local(activations, out_grad, gate_weight, up_weight, down_weight):
    n_blk, n_tensor = lax.axis_size("blk"), lax.axis_size("tensor")
    hidden = gate_weight.shape[2]
    step = -(-hidden // 8) * 8
    pairs = n_tensor == 2 and n_blk % 2 == 0
    w_gate, w_up, w_down = gate_weight[0].T, up_weight[0].T, down_weight[0]
    prev_down, prev_gate, prev_up = [from_behind(w, "blk", 1) for w in (w_down, w_gate, w_up)]
    weights = [prev_gate, prev_up]
    if pairs:
        axes = ("blk", "tensor")
        swap = [(0, 1), (1, 0)]
        on_chip = [(2 * b + j, 2 * (b + 1) + j) for b in range(0, n_blk, 2) for j in range(2)]
        across = [(2 * b + j, 2 * b + 1 - j) for b in range(0, n_blk, 2) for j in range(2)]
        other_gate, other_up = [lax.ppermute(w, "tensor", swap) for w in (w_gate, w_up)]

    w_gu, own_grads, own_hidden = own_meeting(activations, out_grad, w_gate, w_up, w_down, step)
    grad_hidden = grad_hidden_of(out_grad, prev_down, own_grads)
    early, late, prev_gu, *grads = second_meeting(
        activations,
        out_grad,
        grad_hidden,
        own_grads,
        weights,
        lax.axis_index("tensor"),
        2 if pairs else 1,
    )
    back_early, back_late = [from_behind(t, "blk", -1) for t in (early, late)]
    sums_early, sums_late = own_sums(activations, out_grad, own_hidden, own_grads, back_early)
    if pairs:
        mine, sent = grads
        prev_other_even = lax.ppermute(prev_gu, axes, across)
        theirs = lax.ppermute(sent, "tensor", swap)
        other_gu = stack(other_gate, other_up, step, theirs)
        prev_other_odd = lax.ppermute(other_gu, axes, on_chip)
        mine_partial, part, done = ready_part(mine, w_gu, prev_gu, theirs, other_gu, sums_late)
    else:
        done = prev_gu
    total_down, total_gate = totals(sums_early, back_early, 2, hidden, activations)
    if pairs:
        in_grad, total_up = last_part(
            mine_partial,
            part,
            theirs,
            prev_other_even,
            prev_other_odd,
            sums_late,
            back_late,
            hidden,
            total_gate,
        )
    else:
        after = in_grad_of(activations, (grads, [[w_gu], [prev_gu]]))
        in_grad = lax.psum_scatter(after, "tensor", scatter_dimension=0, tiled=True)
        [total_up] = totals(sums_late, back_late, 1, hidden, after)
    return (
        in_grad,
        total_gate.transpose(1, 2, 0),
        total_up.transpose(1, 2, 0),
        total_down.transpose(1, 0, 2),
    )


def solution(mesh):
    in_specs = (
        P("blk", None),
        P("blk", None),
        P("blk", None, "tensor"),
        P("blk", None, "tensor"),
        P("blk", "tensor", None),
    )
    out_specs = (
        P(("blk", "tensor"), None),
        P("blk", None, "tensor"),
        P("blk", None, "tensor"),
        P("blk", "tensor", None),
    )
    return jax.shard_map(local, mesh=mesh, in_specs=in_specs, out_specs=out_specs, check_vma=False)
```
